512 devices in a mesh: fib: 32 (over z_lo, x, core), oth: 16 (over z_hi, y).
Axes of the slice: x: 4, y: 4, z: 16 (z_hi: 4, z_lo: 4; z = z_hi * 4 + z_lo), core: 2. Of those that a mesh axis runs over, the one named last changes fastest.
Arguments:
- slab: float32 [1024, 16, 32, 128], P('fib', 'oth')
- start_basis: bfloat16 [1024, 128], replicated, may hold values from -6 to 6
Outputs:
- core: float32 [128, 16, 32, 128], P(None, 'oth', 'fib')
The draws below stay inside these ranges and needn't reach their ends.
All inputs are finite; a program needn't handle non-finite values.
Results may differ from the reference program's by a relative error of at most 0.0023.
Values may be sent and summed in bfloat16 or wider, within the bound.
A program may use at most 64 MiB of HBM per device.

```python
import math
import jax
import jax.numpy as jnp
from jax import lax

I1 = 1024
R = 128
ITERS = 3
CELLS = 128
YB = 16
YF = 32


def draw_slab(key, part):
    key = jax.random.fold_in(key, 7)
    keys = jax.random.split(key, 5)
    shape = (I1, YB, YF, CELLS)
    group = jnp.arange(I1) % R
    amplitude = jax.random.uniform(keys[0], (I1,), jnp.float32, 0.5, 1.5)
    strength = jnp.exp(jax.random.uniform(keys[1], (R,), jnp.float32, math.log(0.6), math.log(1.2)))
    shared = jax.random.normal(keys[2], (R, YB, YF, CELLS), jnp.float32)
    noise = jax.random.normal(keys[3], shape, jnp.float32)
    lower, upper = (0.7, 1.4)
    rough = jnp.exp(jax.random.uniform(keys[4], (YB, YF, CELLS), jnp.float32, math.log(lower), math.log(upper)))
    place = (jnp.arange(YF)[None, :] * YB + jnp.arange(YB)[:, None]).astype(jnp.float32) / (YB * YF)
    rising = jnp.exp(math.log(3.0) * place)[:, :, None] * rough
    weight = (amplitude * strength[group])[:, None, None, None]
    return rising[None] * (weight * shared[group] + noise)


def scatter_about(own_key, extent, scale, limit, kind=jnp.bfloat16):
    drawn = scale * jax.random.normal(own_key, extent, jnp.float32)
    return jnp.clip(drawn, min=-limit, max=limit).astype(kind)


def setup_inputs(seed: int = 0) -> dict:
    key_list = jax.random.split(jax.random.key(seed), 3)
    slab = draw_slab(jax.random.fold_in(key_list[2], 71), 0)
    start_basis = scatter_about(key_list[1], (I1, R), 1.0, 6.0)
    return {"slab": slab, "start_basis": start_basis}


def orthonormal(image):
    square = jnp.dot(image.T, image, precision=lax.Precision.HIGHEST)
    low = jnp.linalg.cholesky(square)
    return lax.linalg.triangular_solve(low, image, left_side=False, lower=True, transpose_a=True)

def reference(slab, start_basis):
    flat = slab.astype(jnp.bfloat16).reshape(I1, YB * YF * CELLS)
    gram = jnp.dot(flat.astype(jnp.float32), flat.T.astype(jnp.float32), preferred_element_type=jnp.float32)
    basis = start_basis.astype(jnp.float32)
    for step in range(ITERS):
        image = jnp.dot(gram, basis, precision=lax.Precision.HIGHEST)
        basis = orthonormal(image)
    narrow = basis.astype(jnp.bfloat16)
    core = jnp.dot(narrow.T.astype(jnp.float32), flat.astype(jnp.float32), preferred_element_type=jnp.float32)
    return core.reshape(R, YB, YF, CELLS)
```

```python
import functools

import jax
import jax.numpy as jnp
from jax import lax
from jax.experimental import pallas as pl
from jax.experimental.pallas import tpu as pltpu
from jax.sharding import PartitionSpec as P

ITERS = 3
RANK = 128
CELLS = 128
CHUNK = 8
GRID = dict(zl=4, x=4, c=2, zh=4, y=4)
MESH = pl.DeviceIdType.MESH
F32 = jnp.float32
BF16 = jnp.bfloat16


def thirds(a):
    high = a.astype(BF16)
    rest = a - high.astype(F32)
    mid = rest.astype(BF16)
    return high, mid, (rest - mid.astype(F32)).astype(BF16)


def sublane(v, s):
    return jnp.broadcast_to(v[s : s + 1, :], v.shape)


def panel_step(b, work, inverse):
    base = pl.multiple_of(b * 8, 8)
    left = work[pl.ds(base, 8), 0:RANK]
    right = work[pl.ds(base, 8), RANK : 2 * RANK]
    turned = pltpu.roll(left, RANK - base, 1)
    cols = [jnp.broadcast_to(turned[:, s : s + 1], (8, RANK)) for s in range(8)]
    row = lax.broadcasted_iota(jnp.int32, (8, RANK), 0)
    lane = lax.broadcasted_iota(jnp.int32, (8, RANK), 1)
    pivots = jnp.zeros((8, RANK), F32)
    for s in range(8):
        pivot = sublane(cols[s], s)
        pivots = jnp.where(row == s, pivot, pivots)
        if s < 7:
            factor = jnp.where(row > s, cols[s] * (1.0 / pivot), 0.0)
            for u in range(s + 1, 8):
                cols[u] = cols[u] - factor * sublane(cols[u], s)
            left = left - factor * sublane(left, s)
            right = right - factor * sublane(right, s)
    inverse[pl.ds(base, 8), :] = right * lax.rsqrt(pivots)
    factors = jnp.where(lane >= base + 8, left * (1.0 / pivots), 0.0)
    fh, fm, fl = [t.astype(F32) for t in thirds(factors)]
    rh, rm, rl = [t.astype(F32) for t in thirds(jnp.concatenate([left, right], axis=1))]
    tall = jnp.concatenate([fh, fh, fm, fh, fl, fm], axis=0).astype(BF16)
    wide = jnp.concatenate([rh, rm, rh, rl, rh, rm], axis=0).astype(BF16)
    work[...] = work[...] - lax.dot_general(
        tall, wide, (((0,), (0,)), ((), ())), preferred_element_type=F32
    )


def start_factor(image, work):
    work[:, 0:RANK] = lax.dot_general(
        image, image, (((0,), (0,)), ((), ())),
        preferred_element_type=F32, precision=lax.Precision.HIGHEST,
    )
    i0 = lax.broadcasted_iota(jnp.int32, (RANK, RANK), 0)
    i1 = lax.broadcasted_iota(jnp.int32, (RANK, RANK), 1)
    work[:, RANK : 2 * RANK] = (i0 == i1).astype(F32)


def to_unit(image):
    return image * (1.0 / jnp.max(jnp.abs(image)))


def kernel(
    grid, slab, start, out,
    stage, send, flat, part, from_core, summed, from_y, chunks, from_zl, from_zh, own, mine,
    image, images, work, inverse,
    load_sem, a_send, a_recv, x_send, x_recv, c_send, c_recv, y_send, y_recv,
    zl_send, zl_recv, zh_send, zh_recv, g_send, g_recv, p_send, p_recv, local_sem,
):
    nzl, nx, nc, nzh, ny = (grid[k] for k in ("zl", "x", "c", "zh", "y"))
    rows = stage.shape[1]
    fib, oth = lax.axis_index("fib"), lax.axis_index("oth")
    c = lax.rem(fib, nc)
    x = lax.rem(lax.div(fib, nc), nx)
    zl = lax.div(fib, nc * nx)
    y = lax.rem(oth, ny)
    zh = lax.div(oth, ny)

    def device(dzl=0, dx=0, dc=0, dzh=0, dy=0):
        f = (lax.rem(zl + dzl, nzl) * nx + lax.rem(x + dx, nx)) * nc + lax.rem(c + dc, nc)
        o = lax.rem(zh + dzh, nzh) * ny + lax.rem(y + dy, ny)
        return (f, o)

    def copy(src, dst, ssem, rsem, to):
        return pltpu.make_async_remote_copy(
            src_ref=src, dst_ref=dst, send_sem=ssem, recv_sem=rsem,
            device_id=to, device_id_type=MESH,
        )

    run = [(dz, dc) for dz in range(nzl) for dc in range(nc) if dz or dc]
    plane = [(dx, dy) for dx in range(nx) for dy in range(ny) if dx or dy]

    loads = []
    for dz in range(nzl):
        to_zl = lax.rem(zl + dz, nzl)
        load = pltpu.make_async_copy(slab.at[:, to_zl], stage.at[dz], load_sem.at[dz])
        load.start()
        loads.append(load)

    barrier = pltpu.get_barrier_semaphore()
    peers = [device(dzh=k) for k in range(1, nzh)]
    peers += [device(dzl=dz, dc=dc) for dz, dc in run]
    peers += [device(dx=dx, dy=dy) for dx, dy in plane]
    for peer in peers:
        pl.semaphore_signal(barrier, inc=1, device_id=peer, device_id_type=MESH)

    for dz in range(nzl):
        loads[dz].wait()
        for px in range(nx):
            v0 = stage[dz, :, px * nc, :]
            v1 = stage[dz, :, px * nc + 1, :]
            same = jnp.where(c == 0, v0, v1).astype(BF16)
            other = jnp.where(c == 0, v1, v0).astype(BF16)
            send[dz, 0, :, px * CELLS : (px + 1) * CELLS] = same
            send[dz, 1, :, px * CELLS : (px + 1) * CELLS] = other

    pl.semaphore_wait(barrier, len(peers))

    started = []
    here = flat.at[pl.ds(pl.multiple_of(fib * rows, rows), rows), :]
    keep = pltpu.make_async_copy(send.at[0, 0], here, local_sem)
    keep.start()
    first = []
    for dz, dc in reversed(run):
        cp = copy(send.at[dz, dc], here, a_send.at[dz, dc], a_recv.at[dz, dc], device(dzl=dz, dc=dc))
        cp.start()
        first.append(cp)
    forwards = []

    def forward(dz, dc, src):
        block = (lax.rem(zl + nzl - dz, nzl) * nx + x) * nc + lax.rem(c + nc - dc, nc)
        dst = flat.at[pl.ds(pl.multiple_of(block * rows, rows), rows), :]
        for dx in range(1, nx):
            cp = copy(
                dst if src is None else src, dst,
                x_send.at[dx, dz, dc], x_recv.at[dx, dz, dc], device(dx=dx),
            )
            cp.start()
            forwards.append(cp)

    forward(0, 0, send.at[0, 0])
    keep.wait()
    for (dz, dc), cp in zip(run, reversed(first)):
        cp.wait_recv()
        forward(dz, dc, None)
    for cp in forwards:
        cp.wait_recv()
    started += first + forwards

    tops = [
        flat[pl.ds(pl.multiple_of((q * nx + x) * nc * rows, nc * rows), nc * rows), :]
        for q in range(nzl)
    ]
    gram = lax.dot_general(
        jnp.concatenate(tops, axis=0), flat[...], (((1,), (1,)), ((), ())),
        preferred_element_type=F32,
    )
    part[...] = gram.reshape(part.shape)
    sends = []
    for q in range(ny):
        cp = copy(part.at[q, 1 - c], from_core.at[q], c_send.at[q], c_recv.at[q], device(dc=1))
        cp.start()
        sends.append(cp)
    for cp in sends:
        cp.wait_recv()
    started += sends
    for q in range(ny):
        summed[q] = part[q, c] + from_core[q]
    sends = []
    for d in range(1, ny):
        cp = copy(summed.at[lax.rem(y + d, ny)], from_y.at[y], y_send.at[d], y_recv.at[d], device(dy=d))
        cp.start()
        sends.append(cp)
    from_y[y] = summed[y]
    for cp in sends:
        cp.wait_recv()
    started += sends
    total = from_y[0]
    for q in range(1, ny):
        total = total + from_y[q]
    chunks[...] = total.reshape(chunks.shape)
    sends = []
    for d in range(1, nzl):
        cp = copy(chunks.at[lax.rem(zl + d, nzl)], from_zl.at[zl], zl_send.at[d], zl_recv.at[d], device(dzl=d))
        cp.start()
        sends.append(cp)
    from_zl[zl] = chunks[zl]
    for cp in sends:
        cp.wait_recv()
    started += sends
    total = from_zl[0]
    for q in range(1, nzl):
        total = total + from_zl[q]
    from_zh[zh] = total
    sends = []
    for d in range(1, nzh):
        cp = copy(from_zh.at[zh], from_zh.at[zh], zh_send.at[d], zh_recv.at[d], device(dzh=d))
        cp.start()
        sends.append(cp)
    for cp in sends:
        cp.wait_recv()
    started += sends
    total = from_zh[0]
    for q in range(1, nzh):
        total = total + from_zh[q]
    own[...] = total

    chip = (y * nx + x) * nc * nzl
    tile = chip + c * nzl + zl

    def gather_start(k, value):
        mine[k] = value
        images[k, pl.ds(pl.multiple_of(tile * CHUNK, CHUNK), CHUNK), :] = value
        dst = images.at[k, pl.ds(pl.multiple_of(tile * CHUNK, CHUNK), CHUNK), :]
        cps = []
        for dz, dc in run:
            cp = copy(mine.at[k], dst, g_send.at[k, dz, dc], g_recv.at[k, dz, dc], device(dzl=dz, dc=dc))
            cp.start()
            cps.append(cp)
        return cps

    def gather_spread(k, cps):
        for cp in cps:
            cp.wait_recv()
        size = nc * nzl * CHUNK
        block = images.at[k, pl.ds(pl.multiple_of(chip * CHUNK, size), size), :]
        more = []
        for dx, dy in plane:
            cp = copy(block, block, p_send.at[k, dx, dy], p_recv.at[k, dx, dy], device(dx=dx, dy=dy))
            cp.start()
            more.append(cp)
        return cps, more

    def gather_end(cps, more):
        for cp in more:
            cp.wait_recv()
        for cp in cps + more:
            cp.wait_send()

    cps = gather_start(0, jnp.dot(own[...], start[...].astype(F32), preferred_element_type=F32,
                                  precision=lax.Precision.HIGHEST))
    for cp in started:
        cp.wait_send()
    gather_end(*gather_spread(0, cps))
    image[...] = to_unit(images[0])
    for k in range(1, ITERS):
        cps = gather_start(k, jnp.dot(own[...], image[...], preferred_element_type=F32,
                                      precision=lax.Precision.HIGHEST))
        start_factor(image[...], work)
        lax.fori_loop(0, 2, lambda b, _: (panel_step(b, work, inverse), 0)[1], 0)
        both = gather_spread(k, cps)
        lax.fori_loop(2, RANK // 8, lambda b, _: (panel_step(b, work, inverse), 0)[1], 0)
        gather_end(*both)
        image[...] = to_unit(lax.dot_general(
            images[k], inverse[...], (((1,), (1,)), ((), ())),
            preferred_element_type=F32, precision=lax.Precision.HIGHEST,
        ))
    start_factor(image[...], work)
    lax.fori_loop(0, RANK // 8, lambda b, _: (panel_step(b, work, inverse), 0)[1], 0)
    narrow = lax.dot_general(
        image[...], inverse[...], (((1,), (1,)), ((), ())),
        preferred_element_type=F32, precision=lax.Precision.HIGHEST,
    ).astype(BF16)
    out[...] = lax.dot_general(
        narrow, flat[:, pl.ds(pl.multiple_of(x * CELLS, CELLS), CELLS)],
        (((0,), (0,)), ((), ())), preferred_element_type=F32,
    )


def local(grid, slab, start):
    nzl, nx, nc, nzh, ny = (grid[k] for k in ("zl", "x", "c", "zh", "y"))
    rows = slab.shape[0]
    order = start.shape[0]
    wide = nx * CELLS
    dma = pltpu.SemaphoreType.DMA
    core = pl.pallas_call(
        functools.partial(kernel, grid),
        out_shape=jax.ShapeDtypeStruct((RANK, CELLS), F32),
        in_specs=[pl.BlockSpec(memory_space=pl.ANY), pl.BlockSpec(memory_space=pltpu.VMEM)],
        out_specs=pl.BlockSpec(memory_space=pltpu.VMEM),
        scratch_shapes=[
            pltpu.VMEM((nzl, rows, nx * nc, CELLS), F32),
            pltpu.VMEM((nzl, nc, rows, wide), BF16),
            pltpu.VMEM((order, wide), BF16),
            pltpu.VMEM((ny, nc, rows, order), F32),
            pltpu.VMEM((ny, rows, order), F32),
            pltpu.VMEM((ny, rows, order), F32),
            pltpu.VMEM((ny, rows, order), F32),
            pltpu.VMEM((nzl, CHUNK, order), F32),
            pltpu.VMEM((nzl, CHUNK, order), F32),
            pltpu.VMEM((nzh, CHUNK, order), F32),
            pltpu.VMEM((CHUNK, order), F32),
            pltpu.VMEM((ITERS, CHUNK, RANK), F32),
            pltpu.VMEM((order, RANK), F32),
            pltpu.VMEM((ITERS, order, RANK), F32),
            pltpu.VMEM((RANK, 2 * RANK), F32),
            pltpu.VMEM((RANK, RANK), F32),
            dma((nzl,)),
            dma((nzl, nc)), dma((nzl, nc)),
            dma((nx, nzl, nc)), dma((nx, nzl, nc)),
            dma((ny,)), dma((ny,)),
            dma((ny,)), dma((ny,)),
            dma((nzl,)), dma((nzl,)),
            dma((nzh,)), dma((nzh,)),
            dma((ITERS, nzl, nc)), dma((ITERS, nzl, nc)),
            dma((ITERS, nx, ny)), dma((ITERS, nx, ny)),
            dma(()),
        ],
        compiler_params=pltpu.CompilerParams(
            collective_id=0, has_side_effects=True, vmem_limit_bytes=40 * 2**20
        ),
        name="truncate",
    )(slab.reshape(rows, nzl, nx * nc, CELLS), start)
    return core.reshape(RANK, 1, 1, CELLS)


def solution(mesh, grid=GRID):
    placed = (P("fib", "oth", None, None), P())
    return jax.shard_map(
        functools.partial(local, grid), mesh=mesh, in_specs=placed,
        out_specs=P(None, "oth", "fib", None), check_vma=False,
    )
```

```python
import functools

import jax
import jax.numpy as jnp
from jax import lax
from jax.experimental import pallas as pl
from jax.experimental.pallas import tpu as pltpu
from jax.sharding import PartitionSpec as P

ITERS = 3
RANK = 128
CELLS = 128
CHUNK = 8
GRID = dict(zl=4, x=4, c=2, zh=4, y=4)
MESH = pl.DeviceIdType.MESH
F32 = jnp.float32
BF16 = jnp.bfloat16


def thirds(a):
    high = a.astype(BF16)
    rest = a - high.astype(F32)
    mid = rest.astype(BF16)
    return high, mid, (rest - mid.astype(F32)).astype(BF16)


def sublane(v, s):
    return jnp.broadcast_to(v[s : s + 1, :], v.shape)


def panel_step(b, work, inverse):
    base = pl.multiple_of(b * 8, 8)
    left = work[pl.ds(base, 8), 0:RANK]
    right = work[pl.ds(base, 8), RANK : 2 * RANK]
    turned = pltpu.roll(left, RANK - base, 1)
    cols = [jnp.broadcast_to(turned[:, s : s + 1], (8, RANK)) for s in range(8)]
    row = lax.broadcasted_iota(jnp.int32, (8, RANK), 0)
    lane = lax.broadcasted_iota(jnp.int32, (8, RANK), 1)
    pivots = jnp.zeros((8, RANK), F32)
    for s in range(8):
        pivot = sublane(cols[s], s)
        pivots = jnp.where(row == s, pivot, pivots)
        if s < 7:
            factor = jnp.where(row > s, cols[s] * (1.0 / pivot), 0.0)
            for u in range(s + 1, 8):
                cols[u] = cols[u] - factor * sublane(cols[u], s)
            left = left - factor * sublane(left, s)
            right = right - factor * sublane(right, s)
    inverse[pl.ds(base, 8), :] = right * lax.rsqrt(pivots)
    factors = jnp.where(lane >= base + 8, left * (1.0 / pivots), 0.0)
    fh, fm, fl = [t.astype(F32) for t in thirds(factors)]
    rh, rm, rl = [t.astype(F32) for t in thirds(jnp.concatenate([left, right], axis=1))]
    tall = jnp.concatenate([fh, fh, fm, fh, fl, fm], axis=0).astype(BF16)
    wide = jnp.concatenate([rh, rm, rh, rl, rh, rm], axis=0).astype(BF16)
    work[...] = work[...] - lax.dot_general(
        tall, wide, (((0,), (0,)), ((), ())), preferred_element_type=F32
    )


def start_factor(image, work):
    work[:, 0:RANK] = lax.dot_general(
        image, image, (((0,), (0,)), ((), ())),
        preferred_element_type=F32, precision=lax.Precision.HIGHEST,
    )
    i0 = lax.broadcasted_iota(jnp.int32, (RANK, RANK), 0)
    i1 = lax.broadcasted_iota(jnp.int32, (RANK, RANK), 1)
    work[:, RANK : 2 * RANK] = (i0 == i1).astype(F32)


def to_unit(image):
    return image * (1.0 / jnp.max(jnp.abs(image)))


def kernel(
    grid, slab, start, out,
    stage, basis, send, flat, part, from_core, summed, relay, from_y, chunks, from_zl, from_zh, own,
    small, s_core, s_summed, s_y, s_chunks, s_zl, s_zh,
    mine, image, images, work, inverse,
    load_sem, local_sem, a_send, a_recv, x_send, x_recv, c_send, c_recv, r_send, r_recv, y_send, y_recv,
    zl_send, zl_recv, zh_send, zh_recv, sc_send, sc_recv, sy_send, sy_recv, sl_send, sl_recv, sh_send, sh_recv,
    g_send, g_recv, p_send, p_recv, q_send, q_recv,
):
    nzl, nx, nc, nzh, ny = (grid[k] for k in ("zl", "x", "c", "zh", "y"))
    rows = stage.shape[1]
    deep = summed.shape[1]
    half = deep // 2
    fib, oth = lax.axis_index("fib"), lax.axis_index("oth")
    c = lax.rem(fib, nc)
    x = lax.rem(lax.div(fib, nc), nx)
    zl = lax.div(fib, nc * nx)
    y = lax.rem(oth, ny)
    zh = lax.div(oth, ny)

    def device(dzl=0, dx=0, dc=0, dzh=0, dy=0):
        f = (lax.rem(zl + dzl, nzl) * nx + lax.rem(x + dx, nx)) * nc + lax.rem(c + dc, nc)
        o = lax.rem(zh + dzh, nzh) * ny + lax.rem(y + dy, ny)
        return (f, o)

    started = []

    def copy(src, dst, ssem, rsem, to):
        cp = pltpu.make_async_remote_copy(
            src_ref=src, dst_ref=dst, send_sem=ssem, recv_sem=rsem,
            device_id=to, device_id_type=MESH,
        )
        cp.start()
        started.append(cp)
        return cp

    def landed(cps):
        for cp in cps:
            cp.wait_recv()

    run = [(dz, dc) for dz in range(nzl) for dc in range(nc)]
    plane = [(dx, dy) for dx in range(nx) for dy in range(ny) if dx or dy]

    loads = []
    for dz in range(nzl):
        to_zl = lax.rem(zl + dz, nzl)
        load = pltpu.make_async_copy(slab.at[:, to_zl], stage.at[dz], load_sem.at[dz])
        load.start()
        loads.append(load)
    load_basis = pltpu.make_async_copy(start, basis, load_sem.at[nzl])
    load_basis.start()

    barrier = pltpu.get_barrier_semaphore()
    peers = [device(dzh=k) for k in range(1, nzh)]
    peers += [device(dzl=dz, dc=dc) for dz, dc in run[1:]]
    peers += [device(dx=dx, dy=dy) for dx, dy in plane]
    for peer in peers:
        pl.semaphore_signal(barrier, inc=1, device_id=peer, device_id_type=MESH)

    for dz in range(nzl):
        loads[dz].wait()
        for px in range(nx):
            v0 = stage[dz, :, px * nc, :]
            v1 = stage[dz, :, px * nc + 1, :]
            same = jnp.where(c == 0, v0, v1).astype(BF16)
            other = jnp.where(c == 0, v1, v0).astype(BF16)
            send[dz, 0, :, px * CELLS : (px + 1) * CELLS] = same
            send[dz, 1, :, px * CELLS : (px + 1) * CELLS] = other

    pl.semaphore_wait(barrier, len(peers))

    def block(dx, dz, dc):
        b = (lax.rem(zl + nzl - dz, nzl) * nx + lax.rem(x + dx, nx)) * nc + lax.rem(c + nc - dc, nc)
        return flat.at[pl.ds(pl.multiple_of(b * rows, rows), rows), :]

    here = block(0, 0, 0)
    keep = pltpu.make_async_copy(send.at[0, 0], here, local_sem)
    keep.start()
    first = {}
    for dz, dc in run[:0:-1]:
        first[dz, dc] = copy(send.at[dz, dc], here, a_send.at[dz, dc], a_recv.at[dz, dc], device(dzl=dz, dc=dc))
    right, left, more = {}, {}, []

    def onward(p):
        landed([right[p], left[p]])
        if p[1] == 0:
            src = block(nx - 1, *p)
            more.append(copy(src, src, x_send.at[2, *p], x_recv.at[2, *p], device(dx=1)))
        else:
            src = block(1, *p)
            more.append(copy(src, src, x_send.at[2, *p], x_recv.at[2, *p], device(dx=nx - 1)))

    for n, p in enumerate(run):
        src = dst = block(0, *p)
        if n:
            landed([first[p]])
        else:
            src = send.at[0, 0]
        right[p] = copy(src, dst, x_send.at[0, *p], x_recv.at[0, *p], device(dx=1))
        left[p] = copy(src, dst, x_send.at[1, *p], x_recv.at[1, *p], device(dx=nx - 1))
        if n >= 4:
            onward(run[n - 4])
    for p in run[-4:]:
        onward(p)
    landed(more)
    keep.wait()
    load_basis.wait()

    tops = jnp.concatenate([
        flat[pl.ds(pl.multiple_of(((q * nx + x) * nc + k) * rows, rows), rows), :]
        for k in range(nc) for q in range(nzl)
    ], axis=0)
    inner = lax.dot_general(
        basis[...], flat[...], (((0,), (0,)), ((), ())), preferred_element_type=F32
    )
    first_image = sum(
        lax.dot_general(tops, t, (((1,), (1,)), ((), ())), preferred_element_type=F32)
        for t in thirds(inner)[::-1]
    )
    small[...] = first_image.reshape(small.shape)
    cp = copy(small.at[1 - c], s_core, sc_send, sc_recv, device(dc=1))
    landed([cp])
    s_summed[...] = small[c] + s_core[...]
    s_y[y] = s_summed[y]
    small_y = [
        copy(s_summed.at[lax.rem(y + d, ny)], s_y.at[y], sy_send.at[d], sy_recv.at[d], device(dy=d))
        for d in (2, 1, 3)
    ]

    gram = lax.dot_general(tops, flat[...], (((1,), (1,)), ((), ())), preferred_element_type=F32)
    part[...] = gram.reshape(part.shape)
    across = []
    for d in (2, 1, 3, 0):
        q = lax.rem(y + d, ny)
        across.append((q, copy(part.at[1 - c, q], from_core.at[q], c_send.at[d], c_recv.at[d], device(dc=1))))

    landed(small_y)
    s_chunks[...] = sum(s_y[q] for q in range(ny)).reshape(s_chunks.shape)
    s_zl[zl] = s_chunks[zl]
    small_zl = [
        copy(s_chunks.at[lax.rem(zl + d, nzl)], s_zl.at[zl], sl_send.at[d], sl_recv.at[d], device(dzl=d))
        for d in range(1, nzl)
    ]

    low, high = pl.ds(0, half), pl.ds(half, half)
    nxt, prv, far = (lax.rem(y + d, ny) for d in (1, 3, 2))
    for n, (q, cp) in enumerate(across):
        landed([cp])
        summed[q] = part[c, q] + from_core[q]
        if n == 0:
            up = copy(summed.at[far, low], relay.at[0], r_send.at[0], r_recv.at[0], device(dy=1))
            down = copy(summed.at[far, high], relay.at[1], r_send.at[1], r_recv.at[1], device(dy=3))
        if n == 1:
            direct_up = copy(summed.at[nxt, high], from_y.at[0, high], y_send.at[0], y_recv.at[0], device(dy=1))
        if n == 2:
            direct_down = copy(summed.at[prv, low], from_y.at[1, low], y_send.at[1], y_recv.at[1], device(dy=3))

    landed([up])
    summed[nxt, low] = summed[nxt, low] + relay[0]
    last_up = copy(summed.at[nxt, low], from_y.at[0, low], y_send.at[2], y_recv.at[2], device(dy=1))
    landed([down])
    summed[prv, high] = summed[prv, high] + relay[1]
    last_down = copy(summed.at[prv, high], from_y.at[1, high], y_send.at[3], y_recv.at[3], device(dy=3))
    landed(small_zl)
    s_zh[zh] = sum(s_zl[q] for q in range(nzl))
    small_zh = [
        copy(s_zh.at[zh], s_zh.at[zh], sh_send.at[d], sh_recv.at[d], device(dzh=d))
        for d in range(1, nzh)
    ]

    landed([direct_up, direct_down, last_up, last_down])
    chunks[...] = (summed[y] + (from_y[0] + from_y[1])).reshape(chunks.shape)
    from_zl[zl] = chunks[zl]
    big_zl = [
        copy(chunks.at[lax.rem(zl + d, nzl)], from_zl.at[zl], zl_send.at[d], zl_recv.at[d], device(dzl=d))
        for d in range(1, nzl)
    ]

    def place(dx, dy, core):
        rho = lax.rem(y + dy, ny) * deep
        b = (lax.div(rho, rows) * nx + lax.rem(x + dx, nx)) * nc + core
        return b * rows + lax.rem(rho, rows)

    line = nzl * CHUNK

    def block_of(k, dx, dy, core):
        return images.at[k, pl.ds(pl.multiple_of(place(dx, dy, core), line), line), :]

    def gather_start(k, value):
        mine[k] = value
        where = pl.ds(pl.multiple_of(place(0, 0, c) + zl * CHUNK, CHUNK), CHUNK)
        images[k, where, :] = value
        return [
            copy(mine.at[k], images.at[k, where, :], g_send.at[k, d], g_recv.at[k, d], device(dzl=d))
            for d in range(1, nzl)
        ]

    def gather_spread(k, cps):
        landed(cps)
        src = block_of(k, 0, 0, c)
        spread = {
            (dx, dy): copy(src, src, p_send.at[k, dx, dy], p_recv.at[k, dx, dy], device(dx=dx, dy=dy))
            for dx, dy in sorted(plane, key=lambda p: -min(p[0], nx - p[0]) - min(p[1], ny - p[1]))
        }
        return spread, [copy(src, src, q_send.at[k, 0, 0], q_recv.at[k, 0, 0], device(dc=1))]

    def gather_end(k, spread, last):
        for dx, dy in sorted(plane, key=lambda p: min(p[0], nx - p[0]) + min(p[1], ny - p[1])):
            landed([spread[dx, dy]])
            src = block_of(k, nx - dx, ny - dy, c)
            last.append(copy(src, src, q_send.at[k, dx, dy], q_recv.at[k, dx, dy], device(dc=1)))
        landed(last)

    def factor(k0, k1):
        lax.fori_loop(k0, k1, lambda b, _: (panel_step(b, work, inverse), 0)[1], 0)

    landed(small_zh)
    cps = gather_start(0, sum(s_zh[q] for q in range(nzh)))
    landed(big_zl)
    from_zh[zh] = sum(from_zl[q] for q in range(nzl))
    big_zh = [
        copy(from_zh.at[zh], from_zh.at[zh], zh_send.at[d], zh_recv.at[d], device(dzh=d))
        for d in range(1, nzh)
    ]
    gather_end(0, *gather_spread(0, cps))
    image[...] = to_unit(images[0])
    start_factor(image[...], work)
    landed(big_zh)
    own[...] = sum(from_zh[q] for q in range(nzh))
    for k in range(1, ITERS):
        cps = gather_start(k, jnp.dot(own[...], image[...], preferred_element_type=F32,
                                      precision=lax.Precision.HIGHEST))
        if k > 1:
            start_factor(image[...], work)
        factor(0, 4 if k == 1 else 2)
        both = gather_spread(k, cps)
        factor(4 if k == 1 else 2, RANK // 8)
        gather_end(k, *both)
        image[...] = to_unit(lax.dot_general(
            images[k], inverse[...], (((1,), (1,)), ((), ())),
            preferred_element_type=F32, precision=lax.Precision.HIGHEST,
        ))
    start_factor(image[...], work)
    factor(0, RANK // 8)
    for cp in started:
        cp.wait_send()
    narrow = lax.dot_general(
        image[...], inverse[...], (((1,), (1,)), ((), ())),
        preferred_element_type=F32, precision=lax.Precision.HIGHEST,
    ).astype(BF16)
    out[...] = lax.dot_general(
        narrow, flat[:, pl.ds(pl.multiple_of(x * CELLS, CELLS), CELLS)],
        (((0,), (0,)), ((), ())), preferred_element_type=F32,
    )


def local(grid, slab, start):
    nzl, nx, nc, nzh, ny = (grid[k] for k in ("zl", "x", "c", "zh", "y"))
    rows = slab.shape[0]
    order = start.shape[0]
    wide = nx * CELLS
    deep = nzl * rows // ny
    dma = pltpu.SemaphoreType.DMA
    vmem = pltpu.VMEM
    core = pl.pallas_call(
        functools.partial(kernel, grid),
        out_shape=jax.ShapeDtypeStruct((RANK, CELLS), F32),
        in_specs=[pl.BlockSpec(memory_space=pltpu.HBM)] * 2,
        out_specs=pl.BlockSpec(memory_space=pltpu.VMEM),
        scratch_shapes=[
            vmem((nzl, rows, nx * nc, CELLS), F32),
            vmem((order, RANK), BF16),
            vmem((nzl, nc, rows, wide), BF16),
            vmem((order, wide), BF16),
            vmem((nc, ny, deep, order), F32),
            vmem((ny, deep, order), F32),
            vmem((ny, deep, order), F32),
            vmem((2, deep // 2, order), F32),
            vmem((2, deep, order), F32),
            vmem((nzl, CHUNK, order), F32),
            vmem((nzl, CHUNK, order), F32),
            vmem((nzh, CHUNK, order), F32),
            vmem((CHUNK, order), F32),
            vmem((nc, ny, deep, RANK), F32),
            vmem((ny, deep, RANK), F32),
            vmem((ny, deep, RANK), F32),
            vmem((ny, deep, RANK), F32),
            vmem((nzl, CHUNK, RANK), F32),
            vmem((nzl, CHUNK, RANK), F32),
            vmem((nzh, CHUNK, RANK), F32),
            vmem((ITERS, CHUNK, RANK), F32),
            vmem((order, RANK), F32),
            vmem((ITERS, order, RANK), F32),
            vmem((RANK, 2 * RANK), F32),
            vmem((RANK, RANK), F32),
            dma((nzl + 1,)), dma(()),
            dma((nzl, nc)), dma((nzl, nc)),
            dma((3, nzl, nc)), dma((3, nzl, nc)),
            dma((ny,)), dma((ny,)),
            dma((2,)), dma((2,)),
            dma((4,)), dma((4,)),
            dma((nzl,)), dma((nzl,)),
            dma((nzh,)), dma((nzh,)),
            dma(()), dma(()),
            dma((ny,)), dma((ny,)),
            dma((nzl,)), dma((nzl,)),
            dma((nzh,)), dma((nzh,)),
            dma((ITERS, nzl)), dma((ITERS, nzl)),
            dma((ITERS, nx, ny)), dma((ITERS, nx, ny)),
            dma((ITERS, nx, ny)), dma((ITERS, nx, ny)),
        ],
        compiler_params=pltpu.CompilerParams(
            collective_id=0, has_side_effects=True, vmem_limit_bytes=40 * 2**20
        ),
        name="truncate",
    )(slab.reshape(rows, nzl, nx * nc, CELLS), start)
    return core.reshape(RANK, 1, 1, CELLS)


def solution(mesh, grid=GRID):
    placed = (P("fib", "oth", None, None), P())
    return jax.shard_map(
        functools.partial(local, grid), mesh=mesh, in_specs=placed,
        out_specs=P(None, "oth", "fib", None), check_vma=False,
    )
```

```python
import functools

import jax
import jax.numpy as jnp
from jax import lax
from jax.experimental import pallas as pl
from jax.experimental.pallas import tpu as pltpu
from jax.sharding import PartitionSpec as P

ITERS = 3
RANK = 128
CELLS = 128
CHUNK = 8
RELAYED = 4
GRID = dict(zl=4, x=4, c=2, zh=4, y=4)
MESH = pl.DeviceIdType.MESH
F32 = jnp.float32
BF16 = jnp.bfloat16


def thirds(a):
    high = a.astype(BF16)
    rest = a - high.astype(F32)
    mid = rest.astype(BF16)
    return high, mid, (rest - mid.astype(F32)).astype(BF16)


PANEL = 16
TILES = PANEL // 8


def panel_step(b, work, inverse):
    fixed = isinstance(b, int)
    base = b * PANEL if fixed else pl.multiple_of(b * PANEL, PANEL)
    left = work[pl.ds(base, PANEL), 0:RANK]
    right = work[pl.ds(base, PANEL), RANK : 2 * RANK]
    turned, at = (left, base) if fixed else (pltpu.roll(left, RANK - base, 1), 0)
    row = lax.broadcasted_iota(jnp.int32, (8, RANK), 0)
    tiles = []
    for t in range(TILES):
        rows = slice(8 * t, 8 * t + 8)
        cols = [jnp.broadcast_to(turned[rows, at + s : at + s + 1], (8, RANK)) for s in range(PANEL)]
        tiles.append(jnp.stack(cols + [left[rows], right[rows]]))
    pivots = [jnp.ones((8, RANK), F32) for _ in range(TILES)]
    for s in range(PANEL):
        ts, ss = divmod(s, 8)
        pivot = jnp.broadcast_to(tiles[ts][0, ss : ss + 1, :], (8, RANK))
        pivots[ts] = jnp.where(row == ss, pivot, pivots[ts])
        over = 1.0 / pivot
        lead = jnp.broadcast_to(tiles[ts][1:, ss : ss + 1, :], (PANEL + 1 - s, 8, RANK))
        for t in range(TILES):
            rest = tiles[t][1:]
            if t >= ts:
                factor = tiles[t][0] * over
                if t == ts:
                    factor = jnp.where(row > ss, factor, 0.0)
                rest = rest - factor[None] * lead
            tiles[t] = rest
    left = jnp.concatenate([tile[0] for tile in tiles], axis=0)
    right = jnp.concatenate([tile[1] for tile in tiles], axis=0)
    pivots = jnp.concatenate(pivots, axis=0)
    inverse[pl.ds(base, PANEL), :] = right * lax.rsqrt(pivots)
    if fixed and base + PANEL == RANK:
        return
    lane = lax.broadcasted_iota(jnp.int32, (PANEL, RANK), 1)
    factors = jnp.where(lane >= base + PANEL, left * (1.0 / pivots), 0.0)
    fh, fm, fl = thirds(factors)
    rh, rm, rl = thirds(jnp.concatenate([left, right], axis=1))
    tall = jnp.concatenate([fh, fh, fm, fh, fl, fm], axis=0)
    wide = jnp.concatenate([rh, rm, rh, rl, rh, rm], axis=0)
    change = lax.dot_general(tall, wide, (((0,), (0,)), ((), ())), preferred_element_type=F32)
    if fixed:
        work[base + PANEL :, :] = work[base + PANEL :, :] - change[base + PANEL :]
    else:
        work[...] = work[...] - change


def start_factor(image, work):
    work[:, 0:RANK] = lax.dot_general(
        image, image, (((0,), (0,)), ((), ())),
        preferred_element_type=F32, precision=lax.Precision.HIGHEST,
    )
    i0 = lax.broadcasted_iota(jnp.int32, (RANK, RANK), 0)
    i1 = lax.broadcasted_iota(jnp.int32, (RANK, RANK), 1)
    work[:, RANK : 2 * RANK] = (i0 == i1).astype(F32)


def to_unit(image):
    return image * (1.0 / jnp.max(jnp.abs(image)))


def kernel(
    grid, slab, start, out,
    stage, basis, send, flat, part, from_core, summed, from_y, chunks, from_zl, from_zh, own,
    small, s_in, s_zh, mine, image, images, work, inverse,
    load_sem, local_sem, a_send, a_recv, x_send, x_recv, c_send, c_recv, y_send, y_recv,
    zl_send, zl_recv, zh_send, zh_recv, o_send, o_recv, si_send, si_recv, sh_send, sh_recv,
    g_send, g_recv, p_send, p_recv, q_send, q_recv, near_sem, far_sem,
):
    nzl, nx, nc, nzh, ny = (grid[k] for k in ("zl", "x", "c", "zh", "y"))
    rows = stage.shape[1]
    deep = summed.shape[2]
    wide = part.shape[4]
    fib, oth = lax.axis_index("fib"), lax.axis_index("oth")
    c = lax.rem(fib, nc)
    x = lax.rem(lax.div(fib, nc), nx)
    zl = lax.div(fib, nc * nx)
    y = lax.rem(oth, ny)
    zh = lax.div(oth, ny)

    def device(dzl=0, dx=0, dc=0, dzh=0, dy=0):
        f = (lax.rem(zl + dzl, nzl) * nx + lax.rem(x + dx, nx)) * nc + lax.rem(c + dc, nc)
        o = lax.rem(zh + dzh, nzh) * ny + lax.rem(y + dy, ny)
        return (f, o)

    def along_z(d):
        z = lax.rem(zh * nzl + zl + d, nzh * nzl)
        f = (lax.rem(z, nzl) * nx + x) * nc + c
        return (f, lax.div(z, nzl) * ny + y)

    started = []

    def copy(src, dst, ssem, rsem, to):
        cp = pltpu.make_async_remote_copy(
            src_ref=src, dst_ref=dst, send_sem=ssem, recv_sem=rsem,
            device_id=to, device_id_type=MESH,
        )
        cp.start()
        started.append(cp)
        return cp

    def landed(cps):
        for cp in cps:
            cp.wait_recv()

    run = [(dz, dc) for dz in range(nzl) for dc in range(nc)]
    plane = [(dx, dy) for dx in range(nx) for dy in range(ny) if dx or dy]

    barrier = pltpu.get_barrier_semaphore()
    block_peers = [
        (dy, dz, dc) for dy in range(ny) for dz in range(nzl) for dc in range(nc) if dy or dz or dc
    ]
    chained = nzl == 4 and nzh == 4
    peers = [device(dzl=dz, dc=dc, dy=dy) for dy, dz, dc in block_peers]
    peers += [device(dx=dx) for dx in range(1, nx)]
    if chained:
        peers += [along_z(2), along_z(nzl * nzh - 2)]
    else:
        peers += [device(dzh=k) for k in range(1, nzh)]
    for peer in peers:
        pl.semaphore_signal(barrier, inc=1, device_id=peer, device_id_type=MESH)

    loads = []
    for dz in range(nzl):
        to_zl = lax.rem(zl + dz, nzl)
        load = pltpu.make_async_copy(slab.at[:, to_zl], stage.at[dz], load_sem.at[dz])
        load.start()
        loads.append(load)
    load_basis = pltpu.make_async_copy(start, basis, load_sem.at[nzl])
    load_basis.start()

    def block(dx, dz, dc):
        b = (lax.rem(zl + nzl - dz, nzl) * nx + lax.rem(x + dx, nx)) * nc + lax.rem(c + nc - dc, nc)
        return flat.at[pl.ds(pl.multiple_of(b * rows, rows), rows), :]

    here = block(0, 0, 0)
    right, left, more = {}, {}, []

    def spread(n, p, src):
        dst = block(0, *p)
        right[p] = copy(src, dst, x_send.at[0, *p], x_recv.at[0, *p], device(dx=1))
        left[p] = copy(src, dst, x_send.at[1, *p], x_recv.at[1, *p], device(dx=nx - 1))
        if n >= RELAYED:
            more.append(copy(src, dst, x_send.at[2, *p], x_recv.at[2, *p], device(dx=2)))

    def onward(n, p):
        landed([right[p], left[p]])
        if n < RELAYED:
            to, src = (1, block(nx - 1, *p)) if n % 2 == 0 else (nx - 1, block(1, *p))
            more.append(copy(src, src, x_send.at[2, *p], x_recv.at[2, *p], device(dx=to)))

    first = {}
    for dz in range(nzl):
        loads[dz].wait()
        for px in range(nx):
            v0 = stage[dz, :, px * nc, :]
            v1 = stage[dz, :, px * nc + 1, :]
            same = jnp.where(c == 0, v0, v1).astype(BF16)
            other = jnp.where(c == 0, v1, v0).astype(BF16)
            send[dz, 0, :, px * CELLS : (px + 1) * CELLS] = same
            send[dz, 1, :, px * CELLS : (px + 1) * CELLS] = other
        if dz == 0:
            pl.semaphore_wait(barrier, len(peers))
            keep = pltpu.make_async_copy(send.at[0, 0], here, local_sem)
            keep.start()
            spread(0, run[0], send.at[0, 0])
        for dc in range(nc):
            if dz or dc:
                first[dz, dc] = copy(
                    send.at[dz, dc], here, a_send.at[dz, dc], a_recv.at[dz, dc], device(dzl=dz, dc=dc)
                )
    if chained:
        for d in (2, nzl * nzh - 2):
            pl.semaphore_signal(near_sem, inc=1, device_id=along_z(d), device_id_type=MESH)
    for n, p in enumerate(run):
        if n:
            landed([first[p]])
            spread(n, p, block(0, *p))
        if n >= 4:
            onward(n - 4, run[n - 4])
    if chained:
        pl.semaphore_wait(near_sem, 2)
        for d in (nzl, nzl * nzh - nzl):
            pl.semaphore_signal(far_sem, inc=1, device_id=along_z(d), device_id_type=MESH)
    for n in range(len(run) - 4, len(run)):
        onward(n, run[n])
    landed(more)
    keep.wait()
    load_basis.wait()

    tops = jnp.concatenate([
        flat[pl.ds(pl.multiple_of(((q * nx + x) * nc + k) * rows, rows), rows), :]
        for k in range(nc) for q in range(nzl)
    ], axis=0)
    inner = lax.dot_general(
        basis[...], flat[...], (((0,), (0,)), ((), ())), preferred_element_type=F32
    )
    first_image = sum(
        lax.dot_general(tops, t, (((1,), (1,)), ((), ())), preferred_element_type=F32)
        for t in thirds(inner)[::-1]
    )
    small[...] = first_image.reshape(small.shape)
    s_in[0] = small[c, y, zl]
    small_in = []
    for n, (dy, dz, dc) in enumerate(block_peers):
        src = small.at[lax.rem(c + dc, nc), lax.rem(y + dy, ny), lax.rem(zl + dz, nzl)]
        small_in.append(
            copy(src, s_in.at[n + 1], si_send.at[n], si_recv.at[n], device(dzl=dz, dc=dc, dy=dy))
        )

    halves = range(2)
    across = []
    for h in halves:
        gram = lax.dot_general(
            tops, flat[h * wide : (h + 1) * wide, :], (((1,), (1,)), ((), ())),
            preferred_element_type=F32,
        )
        part[h] = gram.reshape(part.shape[1:])
        for d in (2, 1, 3, 0):
            q = lax.rem(y + d, ny)
            across.append((h, d, q, copy(
                part.at[h, 1 - c, q], from_core.at[h, q], c_send.at[h, d], c_recv.at[h, d], device(dc=1)
            )))

    big_y = [[], []]
    for h, d, q, cp in across:
        landed([cp])
        if d == 0:
            from_y[h, y] = part[h, c, q] + from_core[h, q]
        else:
            summed[h, q] = part[h, c, q] + from_core[h, q]
            big_y[h].append(copy(
                summed.at[h, q], from_y.at[h, y], y_send.at[h, d], y_recv.at[h, d], device(dy=d)
            ))

    landed(small_in)
    s_zh[zh] = jnp.sum(s_in[...], axis=0)
    if chained:
        pl.semaphore_wait(far_sem, 2)
    small_zh = [
        copy(s_zh.at[zh], s_zh.at[zh], sh_send.at[d], sh_recv.at[d], device(dzh=d))
        for d in range(1, nzh)
    ]

    big_zl, big_zh, big_own = [[], []], [[], []], [[], []]

    def after_y(h):
        landed(big_y[h])
        chunks[h] = sum(from_y[h, q] for q in range(ny)).reshape(chunks.shape[1:])
        from_zl[h, zl] = chunks[h, zl]
        for d in range(1, nzl):
            big_zl[h].append(copy(
                chunks.at[h, lax.rem(zl + d, nzl)], from_zl.at[h, zl],
                zl_send.at[h, d], zl_recv.at[h, d], device(dzl=d),
            ))

    def after_zl(h):
        landed(big_zl[h])
        from_zh[h, zh] = sum(from_zl[h, q] for q in range(nzl))
        for d in range(1, nzh):
            big_zh[h].append(copy(
                from_zh.at[h, zh], from_zh.at[h, zh],
                zh_send.at[h, d], zh_recv.at[h, d], device(dzh=d),
            ))

    def after_zh(h):
        landed(big_zh[h])
        own[h, zl] = sum(from_zh[h, q] for q in range(nzh))
        for d in range(1, nzl):
            big_own[h].append(copy(
                own.at[h, zl], own.at[h, zl], o_send.at[h, d], o_recv.at[h, d], device(dzl=d),
            ))

    after_y(0)
    after_y(1)
    after_zl(0)

    def place(dx, dy, core):
        rho = lax.rem(y + dy, ny) * deep
        b = (lax.div(rho, rows) * nx + lax.rem(x + dx, nx)) * nc + core
        return b * rows + lax.rem(rho, rows)

    line = nzl * CHUNK

    def block_of(k, dx, dy, core):
        return images.at[k, pl.ds(pl.multiple_of(place(dx, dy, core), line), line), :]

    def gather_start(k, value):
        mine[k] = value
        where = pl.ds(pl.multiple_of(place(0, 0, c) + zl * CHUNK, CHUNK), CHUNK)
        images[k, where, :] = value
        return [
            copy(mine.at[k], images.at[k, where, :], g_send.at[k, d], g_recv.at[k, d], device(dzl=d))
            for d in range(1, nzl)
        ]

    def gather_spread(k, cps):
        landed(cps)
        src = block_of(k, 0, 0, c)
        spread = {
            (dx, dy): copy(src, src, p_send.at[k, dx, dy], p_recv.at[k, dx, dy], device(dx=dx, dy=dy))
            for dx, dy in sorted(plane, key=lambda p: -min(p[0], nx - p[0]) - min(p[1], ny - p[1]))
        }
        return spread, [copy(src, src, q_send.at[k, 0, 0], q_recv.at[k, 0, 0], device(dc=1))]

    def gather_end(k, spread, last):
        for dx, dy in sorted(plane, key=lambda p: min(p[0], nx - p[0]) + min(p[1], ny - p[1])):
            landed([spread[dx, dy]])
            src = block_of(k, nx - dx, ny - dy, c)
            last.append(copy(src, src, q_send.at[k, dx, dy], q_recv.at[k, dx, dy], device(dc=1)))
        landed(last)

    def factor(k0, k1):
        lax.fori_loop(k0, k1, lambda b, _: (panel_step(b, work, inverse), 0)[1], 0)

    landed(small_zh)
    cps = gather_start(0, sum(s_zh[q] for q in range(nzh)))
    after_zl(1)
    both = gather_spread(0, cps)
    gather_end(0, *both)
    image[...] = to_unit(images[0])
    after_zh(0)
    after_zh(1)

    def times(mat, vec):
        return jnp.dot(mat, vec, preferred_element_type=F32, precision=lax.Precision.HIGHEST)

    for k in range(1, ITERS):
        if k == 1:
            rows_of = times(own[0, zl], image[:wide]) + times(own[1, zl], image[wide:])
            cps = gather_start(k, rows_of)
        else:
            landed(big_own[0] + big_own[1])
            rows_of = sum(times(own[h].reshape(line, wide), image[h * wide : (h + 1) * wide]) for h in halves)
            images[k, pl.ds(pl.multiple_of(place(0, 0, c), line), line), :] = rows_of
            both = gather_spread(k, [])
        start_factor(image[...], work)
        if k == 1:
            both = gather_spread(k, cps)
        factor(0, RANK // PANEL)
        gather_end(k, *both)
        image[...] = to_unit(lax.dot_general(
            images[k], inverse[...], (((1,), (1,)), ((), ())),
            preferred_element_type=F32, precision=lax.Precision.HIGHEST,
        ))
    start_factor(image[...], work)
    for b in range(RANK // PANEL):
        panel_step(b, work, inverse)
    for cp in started:
        cp.wait_send()
    narrow = lax.dot_general(
        image[...], inverse[...], (((1,), (1,)), ((), ())),
        preferred_element_type=F32, precision=lax.Precision.HIGHEST,
    ).astype(BF16)
    out[...] = lax.dot_general(
        narrow, flat[:, pl.ds(pl.multiple_of(x * CELLS, CELLS), CELLS)],
        (((0,), (0,)), ((), ())), preferred_element_type=F32,
    )


def local(grid, slab, start):
    nzl, nx, nc, nzh, ny = (grid[k] for k in ("zl", "x", "c", "zh", "y"))
    rows = slab.shape[0]
    order = start.shape[0]
    wide = order // 2
    deep = nzl * rows // ny
    dma = pltpu.SemaphoreType.DMA
    vmem = pltpu.VMEM
    core = pl.pallas_call(
        functools.partial(kernel, grid),
        out_shape=jax.ShapeDtypeStruct((RANK, CELLS), F32),
        in_specs=[pl.BlockSpec(memory_space=pltpu.HBM)] * 2,
        out_specs=pl.BlockSpec(memory_space=pltpu.VMEM),
        scratch_shapes=[
            vmem((nzl, rows, nx * nc, CELLS), F32),
            vmem((order, RANK), BF16),
            vmem((nzl, nc, rows, nx * CELLS), BF16),
            vmem((order, nx * CELLS), BF16),
            vmem((2, nc, ny, deep, wide), F32),
            vmem((2, ny, deep, wide), F32),
            vmem((2, ny, deep, wide), F32),
            vmem((2, ny, deep, wide), F32),
            vmem((2, nzl, CHUNK, wide), F32),
            vmem((2, nzl, CHUNK, wide), F32),
            vmem((2, nzh, CHUNK, wide), F32),
            vmem((2, nzl, CHUNK, wide), F32),
            vmem((nc, ny, nzl, CHUNK, RANK), F32),
            vmem((nc * ny * nzl, CHUNK, RANK), F32),
            vmem((nzh, CHUNK, RANK), F32),
            vmem((ITERS, CHUNK, RANK), F32),
            vmem((order, RANK), F32),
            vmem((ITERS, order, RANK), F32),
            vmem((RANK, 2 * RANK), F32),
            vmem((RANK, RANK), F32),
            dma((nzl + 1,)), dma(()),
            dma((nzl, nc)), dma((nzl, nc)),
            dma((3, nzl, nc)), dma((3, nzl, nc)),
            dma((2, ny)), dma((2, ny)),
            dma((2, ny)), dma((2, ny)),
            dma((2, nzl)), dma((2, nzl)),
            dma((2, nzh)), dma((2, nzh)),
            dma((2, nzl)), dma((2, nzl)),
            dma((nc * ny * nzl - 1,)), dma((nc * ny * nzl - 1,)),
            dma((nzh,)), dma((nzh,)),
            dma((ITERS, nzl)), dma((ITERS, nzl)),
            dma((ITERS, nx, ny)), dma((ITERS, nx, ny)),
            dma((ITERS, nx, ny)), dma((ITERS, nx, ny)),
            pltpu.SemaphoreType.REGULAR, pltpu.SemaphoreType.REGULAR,
        ],
        compiler_params=pltpu.CompilerParams(
            collective_id=0, has_side_effects=True, vmem_limit_bytes=60 * 2**20
        ),
        name="truncate",
    )(slab.reshape(rows, nzl, nx * nc, CELLS), start)
    return core.reshape(RANK, 1, 1, CELLS)


def solution(mesh, grid=GRID):
    placed = (P("fib", "oth", None, None), P())
    return jax.shard_map(
        functools.partial(local, grid), mesh=mesh, in_specs=placed,
        out_specs=P(None, "oth", "fib", None), check_vma=False,
    )
```

```python
import functools

import jax
import jax.numpy as jnp
from jax import lax
from jax.experimental import pallas as pl
from jax.experimental.pallas import tpu as pltpu
from jax.sharding import PartitionSpec as P

ITERS = 3
RANK = 128
CELLS = 128
CHUNK = 8
GRID = dict(zl=4, x=4, c=2, zh=4, y=4)
MESH = pl.DeviceIdType.MESH
F32 = jnp.float32
BF16 = jnp.bfloat16


def thirds(a):
    high = a.astype(BF16)
    rest = a - high.astype(F32)
    mid = rest.astype(BF16)
    return high, mid, (rest - mid.astype(F32)).astype(BF16)


PANEL = 16
TILES = PANEL // 8


def panel_step(b, work, inverse):
    fixed = isinstance(b, int)
    base = b * PANEL if fixed else pl.multiple_of(b * PANEL, PANEL)
    left = work[pl.ds(base, PANEL), 0:RANK]
    right = work[pl.ds(base, PANEL), RANK : 2 * RANK]
    turned, at = (left, base) if fixed else (pltpu.roll(left, RANK - base, 1), 0)
    row = lax.broadcasted_iota(jnp.int32, (8, RANK), 0)
    tiles = []
    for t in range(TILES):
        rows = slice(8 * t, 8 * t + 8)
        cols = [jnp.broadcast_to(turned[rows, at + s : at + s + 1], (8, RANK)) for s in range(PANEL)]
        tiles.append(jnp.stack(cols + [left[rows], right[rows]]))
    pivots = [jnp.ones((8, RANK), F32) for _ in range(TILES)]
    for s in range(PANEL):
        ts, ss = divmod(s, 8)
        pivot = jnp.broadcast_to(tiles[ts][0, ss : ss + 1, :], (8, RANK))
        pivots[ts] = jnp.where(row == ss, pivot, pivots[ts])
        over = 1.0 / pivot
        lead = jnp.broadcast_to(tiles[ts][1:, ss : ss + 1, :], (PANEL + 1 - s, 8, RANK))
        for t in range(TILES):
            rest = tiles[t][1:]
            if t >= ts:
                factor = tiles[t][0] * over
                if t == ts:
                    factor = jnp.where(row > ss, factor, 0.0)
                rest = rest - factor[None] * lead
            tiles[t] = rest
    left = jnp.concatenate([tile[0] for tile in tiles], axis=0)
    right = jnp.concatenate([tile[1] for tile in tiles], axis=0)
    pivots = jnp.concatenate(pivots, axis=0)
    inverse[pl.ds(base, PANEL), :] = right * lax.rsqrt(pivots)
    if fixed and base + PANEL == RANK:
        return
    lane = lax.broadcasted_iota(jnp.int32, (PANEL, RANK), 1)
    factors = jnp.where(lane >= base + PANEL, left * (1.0 / pivots), 0.0)
    fh, fm, fl = thirds(factors)
    rh, rm, rl = thirds(jnp.concatenate([left, right], axis=1))
    tall = jnp.concatenate([fh, fh, fm, fh, fl, fm], axis=0)
    wide = jnp.concatenate([rh, rm, rh, rl, rh, rm], axis=0)
    change = lax.dot_general(tall, wide, (((0,), (0,)), ((), ())), preferred_element_type=F32)
    if fixed:
        work[base + PANEL :, :] = work[base + PANEL :, :] - change[base + PANEL :]
    else:
        work[...] = work[...] - change


def start_factor(image, work):
    work[:, 0:RANK] = lax.dot_general(
        image, image, (((0,), (0,)), ((), ())),
        preferred_element_type=F32, precision=lax.Precision.HIGHEST,
    )
    i0 = lax.broadcasted_iota(jnp.int32, (RANK, RANK), 0)
    i1 = lax.broadcasted_iota(jnp.int32, (RANK, RANK), 1)
    work[:, RANK : 2 * RANK] = (i0 == i1).astype(F32)


def to_unit(image):
    return image * (1.0 / jnp.max(jnp.abs(image)))


def kernel(
    grid, slab, start, out,
    stage, basis, send, flat, part, from_core, summed, from_y, chunks, from_zl, from_zh, own,
    small, s_in, s_line, mine, image, images, work, inverse,
    load_sem, sent, a_in, x_in, c_in, y_in, zl_in, zh_in, o_in, si_in, sl_in, g_in, p_in, q_in, near_sem, far_sem,
):
    nzl, nx, nc, nzh, ny = (grid[k] for k in ("zl", "x", "c", "zh", "y"))
    rows = stage.shape[1]
    deep = summed.shape[2]
    wide = part.shape[4]
    fib, oth = lax.axis_index("fib"), lax.axis_index("oth")
    c = lax.rem(fib, nc)
    x = lax.rem(lax.div(fib, nc), nx)
    zl = lax.div(fib, nc * nx)
    y = lax.rem(oth, ny)
    zh = lax.div(oth, ny)

    def device(dzl=0, dx=0, dc=0, dzh=0, dy=0):
        f = (lax.rem(zl + dzl, nzl) * nx + lax.rem(x + dx, nx)) * nc + lax.rem(c + dc, nc)
        o = lax.rem(zh + dzh, nzh) * ny + lax.rem(y + dy, ny)
        return (f, o)

    def along_z(d):
        z = lax.rem(zh * nzl + zl + d, nzh * nzl)
        f = (lax.rem(z, nzl) * nx + x) * nc + c
        return (f, lax.div(z, nzl) * ny + y)

    started = []

    def copy(src, dst, rsem, to):
        cp = pltpu.make_async_remote_copy(
            src_ref=src, dst_ref=dst, send_sem=sent, recv_sem=rsem,
            device_id=to, device_id_type=MESH,
        )
        cp.start()
        started.append(cp)
        return cp

    def landed(like, sem):
        pltpu.make_async_copy(like, like, sem).wait()

    run = [(dz, dc) for dz in range(nzl) for dc in range(nc)]
    plane = [(dx, dy) for dx in range(nx) for dy in range(ny) if dx or dy]

    barrier = pltpu.get_barrier_semaphore()
    block_peers = [
        (dy, dz, dc) for dy in range(ny) for dz in range(nzl) for dc in range(nc) if dy or dz or dc
    ]
    line_of = range(1, nzl * nzh)
    chained = nzl == 4 and nzh == 4
    peers = [device(dzl=dz, dc=dc, dy=dy) for dy, dz, dc in block_peers if dy == 0 or not chained]
    peers += [device(dx=dx) for dx in range(1, nx)]
    if chained:
        step_one = [along_z(2), along_z(14), device(dy=1), device(dy=ny - 1)]
        step_two = [along_z(4), along_z(12), device(dy=1), device(dy=ny - 1)]
        peers += step_one
    else:
        peers += [along_z(d) for d in line_of]
    for peer in peers:
        pl.semaphore_signal(barrier, inc=1, device_id=peer, device_id_type=MESH)

    loads = []
    for dz in range(nzl):
        to_zl = lax.rem(zl + dz, nzl)
        load = pltpu.make_async_copy(slab.at[:, to_zl], stage.at[dz], load_sem.at[dz])
        load.start()
        loads.append(load)
    load_basis = pltpu.make_async_copy(start, basis, load_sem.at[nzl])
    load_basis.start()

    halves = range(2)
    cols = nx // 2 * CELLS

    def block(h, dz, dc):
        b = (lax.rem(zl + nzl - dz, nzl) * nx + x) * nc + lax.rem(c + nc - dc, nc)
        return flat.at[h, pl.ds(pl.multiple_of(b * rows, rows), rows), :]

    def along_x(src, dst):
        for dx in (2, 1, 3):
            copy(src, dst, x_in, device(dx=dx))

    for dz in range(nzl):
        loads[dz].wait()
        for px in range(nx):
            h, at = divmod(px * CELLS, cols)
            v0 = stage[dz, :, px * nc, :]
            v1 = stage[dz, :, px * nc + 1, :]
            send[h, dz, 0, :, at : at + CELLS] = jnp.where(c == 0, v0, v1).astype(BF16)
            send[h, dz, 1, :, at : at + CELLS] = jnp.where(c == 0, v1, v0).astype(BF16)
        if dz == 0:
            keeps = [
                pltpu.make_async_copy(send.at[h, 0, 0], block(h, 0, 0), load_sem.at[nzl + 1 + h])
                for h in halves
            ]
            for keep in keeps:
                keep.start()
            pl.semaphore_wait(barrier, len(peers))
            if chained:
                for peer in step_one:
                    pl.semaphore_signal(near_sem, inc=1, device_id=peer, device_id_type=MESH)
            along_x(send.at[0, 0, 0], block(0, 0, 0))
        for dc in range(nc):
            if dz or dc:
                copy(send.at[0, dz, dc], block(0, 0, 0), a_in.at[0, dz, dc], device(dzl=dz, dc=dc))
    for dz, dc in run[1:]:
        copy(send.at[1, dz, dc], block(1, 0, 0), a_in.at[1, dz, dc], device(dzl=dz, dc=dc))
    along_x(send.at[1, 0, 0], block(1, 0, 0))
    for h in halves:
        for p in run[1:]:
            landed(block(h, *p), a_in.at[h, *p])
            along_x(block(h, *p), block(h, *p))
        if h == 0 and chained:
            pl.semaphore_wait(near_sem, len(step_one))
            for peer in step_two:
                pl.semaphore_signal(far_sem, inc=1, device_id=peer, device_id_type=MESH)
    for keep in keeps:
        keep.wait()
    load_basis.wait()
    if chained:
        pl.semaphore_wait(far_sem, len(step_two))
    landed(flat.at[:, pl.ds(0, (nx - 1) * nzl * nc * rows), :], x_in)

    tops = [
        jnp.concatenate([
            flat[h, pl.ds(pl.multiple_of(((q * nx + x) * nc + k) * rows, rows), rows), :]
            for k in range(nc) for q in range(nzl)
        ], axis=0)
        for h in halves
    ]

    def against(a, b):
        return lax.dot_general(a, b, (((1,), (1,)), ((), ())), preferred_element_type=F32)

    first_image = None
    for h in halves:
        inner = lax.dot_general(
            basis[...], flat[h], (((0,), (0,)), ((), ())), preferred_element_type=F32
        )
        for t in thirds(inner):
            term = against(tops[h], t)
            first_image = term if first_image is None else first_image + term
    small[...] = first_image.reshape(small.shape)
    s_in[0] = small[c, y, zl]
    for n, (dy, dz, dc) in enumerate(block_peers):
        src = small.at[lax.rem(c + dc, nc), lax.rem(y + dy, ny), lax.rem(zl + dz, nzl)]
        copy(src, s_in.at[n + 1], si_in, device(dzl=dz, dc=dc, dy=dy))

    for h in halves:
        span = slice(h * wide, (h + 1) * wide)
        part[h] = sum(against(tops[g], flat[g, span, :]) for g in halves).reshape(part.shape[1:])
        for d in (2, 1, 3, 0):
            q = lax.rem(y + d, ny)
            copy(part.at[h, 1 - c, q], from_core.at[h, q], c_in.at[h], device(dc=1))

    for h in halves:
        landed(from_core.at[h], c_in.at[h])
        for d in (2, 1, 3, 0):
            q = lax.rem(y + d, ny)
            if d == 0:
                from_y[h, y] = part[h, c, q] + from_core[h, q]
            else:
                summed[h, q] = part[h, c, q] + from_core[h, q]
                copy(summed.at[h, q], from_y.at[h, y], y_in.at[h], device(dy=d))

    landed(s_in.at[1:], si_in)
    place_z = zh * nzl + zl
    s_line[place_z] = jnp.sum(s_in[...], axis=0)
    for d in sorted(line_of, key=lambda d: -min(d, nzl * nzh - d)):
        copy(s_line.at[place_z], s_line.at[place_z], sl_in, along_z(d))

    def after_y(h):
        landed(from_y.at[h, 1:], y_in.at[h])
        chunks[h] = sum(from_y[h, q] for q in range(ny)).reshape(chunks.shape[1:])
        from_zl[h, zl] = chunks[h, zl]
        for d in range(1, nzl):
            copy(chunks.at[h, lax.rem(zl + d, nzl)], from_zl.at[h, zl], zl_in.at[h], device(dzl=d))

    def after_zl(h):
        landed(from_zl.at[h, 1:], zl_in.at[h])
        from_zh[h, zh] = sum(from_zl[h, q] for q in range(nzl))
        for d in range(1, nzh):
            copy(from_zh.at[h, zh], from_zh.at[h, zh], zh_in.at[h], device(dzh=d))

    def after_zh(h):
        landed(from_zh.at[h, 1:], zh_in.at[h])
        own[h, zl] = sum(from_zh[h, q] for q in range(nzh))
        for d in range(1, nzl):
            copy(own.at[h, zl], own.at[h, zl], o_in, device(dzl=d))

    after_y(0)
    after_y(1)
    after_zl(0)

    def place(dx, dy, core):
        rho = lax.rem(y + dy, ny) * deep
        b = (lax.div(rho, rows) * nx + lax.rem(x + dx, nx)) * nc + core
        return b * rows + lax.rem(rho, rows)

    line = nzl * CHUNK

    def block_of(k, dx, dy, core):
        return images.at[k, pl.ds(pl.multiple_of(place(dx, dy, core), line), line), :]

    def hops(p):
        return min(p[0], nx - p[0]) + min(p[1], ny - p[1])

    def gather_start(k, value):
        mine[k] = value
        where = pl.ds(pl.multiple_of(place(0, 0, c) + zl * CHUNK, CHUNK), CHUNK)
        images[k, where, :] = value
        for d in range(1, nzl):
            copy(mine.at[k], images.at[k, where, :], g_in, device(dzl=d))

    def gather_spread(k):
        src = block_of(k, 0, 0, c)
        for p in sorted(plane, key=lambda p: -hops(p)):
            copy(src, src, p_in.at[k, int(hops(p) > 2)], device(dx=p[0], dy=p[1]))
        copy(src, src, q_in.at[k], device(dc=1))

    def gather_pass(k, far):
        group = [p for p in plane if (hops(p) > 2) == far]
        landed(images.at[k, pl.ds(0, len(group) * line), :], p_in.at[k, int(far)])
        for dx, dy in group:
            src = block_of(k, nx - dx, ny - dy, c)
            copy(src, src, q_in.at[k], device(dc=1))

    def gather_end(k):
        landed(images.at[k, pl.ds(0, nx * ny * line), :], q_in.at[k])

    def factor(k0, k1):
        lax.fori_loop(k0, k1, lambda b, _: (panel_step(b, work, inverse), 0)[1], 0)

    landed(s_line.at[1:], sl_in)
    mine_rows = pl.ds(pl.multiple_of(place(0, 0, c), line), line)
    images[0, mine_rows, :] = sum(
        s_line[q * nzl : (q + 1) * nzl] for q in range(nzh)
    ).reshape(line, RANK)
    gather_spread(0)
    after_zl(1)
    gather_pass(0, False)
    gather_pass(0, True)
    gather_end(0)
    image[...] = to_unit(images[0])
    after_zh(0)
    after_zh(1)

    def times(mat, vec):
        return jnp.dot(mat, vec, preferred_element_type=F32, precision=lax.Precision.HIGHEST)

    for k in range(1, ITERS):
        if k == 1:
            gather_start(k, times(own[0, zl], image[:wide]) + times(own[1, zl], image[wide:]))
            start_factor(image[...], work)
            factor(0, 2)
            landed(images.at[k, pl.ds(0, (nzl - 1) * CHUNK), :], g_in)
            gather_spread(k)
            factor(2, 7)
        else:
            landed(own.at[:, 1:], o_in)
            images[k, mine_rows, :] = sum(
                times(own[h].reshape(line, wide), image[h * wide : (h + 1) * wide]) for h in halves
            )
            gather_spread(k)
            start_factor(image[...], work)
            factor(0, 5)
        gather_pass(k, False)
        factor(7 if k == 1 else 5, RANK // PANEL)
        gather_pass(k, True)
        gather_end(k)
        image[...] = to_unit(lax.dot_general(
            images[k], inverse[...], (((1,), (1,)), ((), ())),
            preferred_element_type=F32, precision=lax.Precision.HIGHEST,
        ))
    start_factor(image[...], work)
    for b in range(RANK // PANEL):
        panel_step(b, work, inverse)
    for cp in started:
        cp.wait_send()
    narrow = lax.dot_general(
        image[...], inverse[...], (((1,), (1,)), ((), ())),
        preferred_element_type=F32, precision=lax.Precision.HIGHEST,
    ).astype(BF16)
    out[...] = lax.dot_general(
        narrow,
        flat[lax.div(x, nx // 2), :, pl.ds(pl.multiple_of(lax.rem(x, nx // 2) * CELLS, CELLS), CELLS)],
        (((0,), (0,)), ((), ())), preferred_element_type=F32,
    )


def local(grid, slab, start):
    nzl, nx, nc, nzh, ny = (grid[k] for k in ("zl", "x", "c", "zh", "y"))
    rows = slab.shape[0]
    order = start.shape[0]
    wide = order // 2
    deep = nzl * rows // ny
    dma = pltpu.SemaphoreType.DMA
    vmem = pltpu.VMEM
    core = pl.pallas_call(
        functools.partial(kernel, grid),
        out_shape=jax.ShapeDtypeStruct((RANK, CELLS), F32),
        in_specs=[pl.BlockSpec(memory_space=pltpu.HBM)] * 2,
        out_specs=pl.BlockSpec(memory_space=pltpu.VMEM),
        scratch_shapes=[
            vmem((nzl, rows, nx * nc, CELLS), F32),
            vmem((order, RANK), BF16),
            vmem((2, nzl, nc, rows, nx // 2 * CELLS), BF16),
            vmem((2, order, nx // 2 * CELLS), BF16),
            vmem((2, nc, ny, deep, wide), F32),
            vmem((2, ny, deep, wide), F32),
            vmem((2, ny, deep, wide), F32),
            vmem((2, ny, deep, wide), F32),
            vmem((2, nzl, CHUNK, wide), F32),
            vmem((2, nzl, CHUNK, wide), F32),
            vmem((2, nzh, CHUNK, wide), F32),
            vmem((2, nzl, CHUNK, wide), F32),
            vmem((nc, ny, nzl, CHUNK, RANK), F32),
            vmem((nc * ny * nzl, CHUNK, RANK), F32),
            vmem((nzh * nzl, CHUNK, RANK), F32),
            vmem((ITERS, CHUNK, RANK), F32),
            vmem((order, RANK), F32),
            vmem((ITERS, order, RANK), F32),
            vmem((RANK, 2 * RANK), F32),
            vmem((RANK, RANK), F32),
            dma((nzl + 3,)), dma(()),
            dma((2, nzl, nc)), dma(()), dma((2,)), dma((2,)), dma((2,)), dma((2,)),
            dma(()), dma(()), dma(()), dma(()), dma((ITERS, 2)), dma((ITERS,)),
            pltpu.SemaphoreType.REGULAR, pltpu.SemaphoreType.REGULAR,
        ],
        compiler_params=pltpu.CompilerParams(
            collective_id=0, has_side_effects=True, vmem_limit_bytes=55104 * 2**10
        ),
        name="truncate",
    )(slab.reshape(rows, nzl, nx * nc, CELLS), start)
    return core.reshape(RANK, 1, 1, CELLS)


def solution(mesh, grid=GRID):
    placed = (P("fib", "oth", None, None), P())
    return jax.shard_map(
        functools.partial(local, grid), mesh=mesh, in_specs=placed,
        out_specs=P(None, "oth", "fib", None), check_vma=False,
    )
```

```python
import functools

import jax
import jax.numpy as jnp
from jax import lax
from jax.experimental import pallas as pl
from jax.experimental.pallas import tpu as pltpu
from jax.sharding import PartitionSpec as P

ITERS = 3
RANK = 128
CELLS = 128
CHUNK = 8
GRID = dict(zl=4, x=4, c=2, zh=4, y=4)
MESH = pl.DeviceIdType.MESH
F32 = jnp.float32
BF16 = jnp.bfloat16


def thirds(a):
    high = a.astype(BF16)
    rest = a - high.astype(F32)
    mid = rest.astype(BF16)
    return high, mid, (rest - mid.astype(F32)).astype(BF16)


PANEL = 16
TILES = PANEL // 8


def panel_step(b, work, inverse):
    fixed = isinstance(b, int)
    base = b * PANEL if fixed else pl.multiple_of(b * PANEL, PANEL)
    left = work[pl.ds(base, PANEL), 0:RANK]
    right = work[pl.ds(base, PANEL), RANK : 2 * RANK]
    turned, at = (left, base) if fixed else (pltpu.roll(left, RANK - base, 1), 0)
    row = lax.broadcasted_iota(jnp.int32, (8, RANK), 0)
    tiles = []
    for t in range(TILES):
        rows = slice(8 * t, 8 * t + 8)
        cols = [jnp.broadcast_to(turned[rows, at + s : at + s + 1], (8, RANK)) for s in range(PANEL)]
        tiles.append(jnp.stack(cols + [left[rows], right[rows]]))
    pivots = [jnp.ones((8, RANK), F32) for _ in range(TILES)]
    for s in range(PANEL):
        ts, ss = divmod(s, 8)
        pivot = jnp.broadcast_to(tiles[ts][0, ss : ss + 1, :], (8, RANK))
        pivots[ts] = jnp.where(row == ss, pivot, pivots[ts])
        over = 1.0 / pivot
        lead = jnp.broadcast_to(tiles[ts][1:, ss : ss + 1, :], (PANEL + 1 - s, 8, RANK))
        for t in range(TILES):
            rest = tiles[t][1:]
            if t >= ts:
                factor = tiles[t][0] * over
                if t == ts:
                    factor = jnp.where(row > ss, factor, 0.0)
                rest = rest - factor[None] * lead
            tiles[t] = rest
    left = jnp.concatenate([tile[0] for tile in tiles], axis=0)
    right = jnp.concatenate([tile[1] for tile in tiles], axis=0)
    pivots = jnp.concatenate(pivots, axis=0)
    inverse[pl.ds(base, PANEL), :] = right * lax.rsqrt(pivots)
    if fixed and base + PANEL == RANK:
        return
    lane = lax.broadcasted_iota(jnp.int32, (PANEL, RANK), 1)
    factors = jnp.where(lane >= base + PANEL, left * (1.0 / pivots), 0.0)
    fh, fm, fl = thirds(factors)
    rh, rm, rl = thirds(jnp.concatenate([left, right], axis=1))
    tall = jnp.concatenate([fh, fh, fm, fh, fl, fm], axis=0)
    wide = jnp.concatenate([rh, rm, rh, rl, rh, rm], axis=0)
    change = lax.dot_general(tall, wide, (((0,), (0,)), ((), ())), preferred_element_type=F32)
    if fixed:
        work[base + PANEL :, :] = work[base + PANEL :, :] - change[base + PANEL :]
    else:
        work[...] = work[...] - change


def start_factor(image, work):
    work[:, 0:RANK] = lax.dot_general(
        image, image, (((0,), (0,)), ((), ())),
        preferred_element_type=F32, precision=lax.Precision.HIGHEST,
    )
    i0 = lax.broadcasted_iota(jnp.int32, (RANK, RANK), 0)
    i1 = lax.broadcasted_iota(jnp.int32, (RANK, RANK), 1)
    work[:, RANK : 2 * RANK] = (i0 == i1).astype(F32)


def to_unit(image):
    return image * (1.0 / jnp.max(jnp.abs(image)))


def kernel(
    grid, slab, start, out,
    stage, basis, send, flat, part, from_core, summed, from_y, chunks, from_zl, from_zh, own,
    small, s_in, s_line, image, images, work, inverse,
    load_sem, sent, a_in, x_in, c_in, y_in, zl_in, zh_in, o_in, si_in, sl_in, p_in, q_in, near_sem, far_sem,
):
    nzl, nx, nc, nzh, ny = (grid[k] for k in ("zl", "x", "c", "zh", "y"))
    rows = stage.shape[1]
    wide = part.shape[4]
    fib, oth = lax.axis_index("fib"), lax.axis_index("oth")
    c = lax.rem(fib, nc)
    x = lax.rem(lax.div(fib, nc), nx)
    zl = lax.div(fib, nc * nx)
    y = lax.rem(oth, ny)
    zh = lax.div(oth, ny)

    def device(dzl=0, dx=0, dc=0, dzh=0, dy=0):
        f = (lax.rem(zl + dzl, nzl) * nx + lax.rem(x + dx, nx)) * nc + lax.rem(c + dc, nc)
        o = lax.rem(zh + dzh, nzh) * ny + lax.rem(y + dy, ny)
        return (f, o)

    def along_z(d):
        z = lax.rem(zh * nzl + zl + d, nzh * nzl)
        f = (lax.rem(z, nzl) * nx + x) * nc + c
        return (f, lax.div(z, nzl) * ny + y)

    started = []

    def copy(src, dst, rsem, to):
        cp = pltpu.make_async_remote_copy(
            src_ref=src, dst_ref=dst, send_sem=sent, recv_sem=rsem,
            device_id=to, device_id_type=MESH,
        )
        cp.start()
        started.append(cp)
        return cp

    def landed(like, sem):
        pltpu.make_async_copy(like, like, sem).wait()

    run = [(dz, dc) for dz in range(nzl) for dc in range(nc)]
    plane = [(dx, dy) for dx in range(nx) for dy in range(ny) if dx or dy]

    barrier = pltpu.get_barrier_semaphore()
    block_peers = [
        (dy, dz, dc) for dy in range(ny) for dz in range(nzl) for dc in range(nc) if dy or dz or dc
    ]
    line_of = range(1, nzl * nzh)
    chained = nzl == 4 and nzh == 4
    peers = [device(dzl=dz, dc=dc, dy=dy) for dy, dz, dc in block_peers if dy == 0 or not chained]
    peers += [device(dx=dx) for dx in range(1, nx)]
    if chained:
        step_one = [along_z(2), along_z(14), device(dy=1), device(dy=ny - 1)]
        step_two = [along_z(4), along_z(12), device(dy=1), device(dy=ny - 1)]
        peers += step_one
    else:
        peers += [along_z(d) for d in line_of]
    for peer in peers:
        pl.semaphore_signal(barrier, inc=1, device_id=peer, device_id_type=MESH)

    loads = []
    for dz in range(nzl):
        to_zl = lax.rem(zl + dz, nzl)
        load = pltpu.make_async_copy(slab.at[:, to_zl], stage.at[dz], load_sem.at[dz])
        load.start()
        loads.append(load)
    for k in range(nx):
        load = pltpu.make_async_copy(start.at[:, k], basis.at[k], load_sem.at[nzl + k])
        load.start()
        loads.append(load)

    def block(dx, dz, dc):
        b = (lax.rem(x + dx, nx) * nzl + lax.rem(zl + nzl - dz, nzl)) * nc + lax.rem(c + nc - dc, nc)
        return flat.at[pl.ds(pl.multiple_of(b * rows, rows), rows), :]

    def quarter(dx):
        return pl.ds(pl.multiple_of(lax.rem(x + dx, nx) * wide, wide), wide)

    here = block(0, 0, 0)
    keep = pltpu.make_async_copy(send.at[0, 0], here, load_sem.at[nzl + nx])
    for dz in range(nzl):
        loads[dz].wait()
        for px in range(nx):
            v0 = stage[dz, :, px * nc, :]
            v1 = stage[dz, :, px * nc + 1, :]
            send[dz, 0, :, px * CELLS : (px + 1) * CELLS] = jnp.where(c == 0, v0, v1).astype(BF16)
            send[dz, 1, :, px * CELLS : (px + 1) * CELLS] = jnp.where(c == 0, v1, v0).astype(BF16)
        if dz == 0:
            keep.start()
            pl.semaphore_wait(barrier, len(peers))
            if chained:
                for peer in step_one:
                    pl.semaphore_signal(near_sem, inc=1, device_id=peer, device_id_type=MESH)
        for dc in range(nc):
            if dz or dc:
                copy(send.at[dz, dc], here, a_in.at[dz, dc], device(dzl=dz, dc=dc))
        if dz == 0:
            copy(send.at[0, 0], here, x_in.at[0], device(dx=1))
            copy(send.at[0, 0], here, x_in.at[1], device(dx=nx - 1))
    for p in run[1:]:
        piece = block(0, *p)
        landed(piece, a_in.at[p])
        copy(piece, piece, x_in.at[0], device(dx=1))
        copy(piece, piece, x_in.at[1], device(dx=nx - 1))
    if chained:
        pl.semaphore_wait(near_sem, len(step_one))
        for peer in step_two:
            pl.semaphore_signal(far_sem, inc=1, device_id=peer, device_id_type=MESH)
    keep.wait()
    for load in loads[nzl:]:
        load.wait()

    def against(a, b):
        return lax.dot_general(a, b, (((1,), (1,)), ((), ())), preferred_element_type=F32)

    tops = jnp.concatenate([
        flat[pl.ds(pl.multiple_of(((x * nzl + q) * nc + k) * rows, rows), rows), :]
        for k in range(nc) for q in range(nzl)
    ], axis=0)

    def gram(d):
        part[d] = against(tops, flat[quarter(d), :]).reshape(part.shape[1:])
        copy(part.at[d, 1 - c], from_core.at[d], c_in.at[d], device(dc=1))

    def after_core(d):
        landed(from_core.at[d], c_in.at[d])
        for dy in (2, 1, 3, 0):
            q = lax.rem(y + dy, ny)
            if dy == 0:
                from_y[d, y] = part[d, c, q] + from_core[d, q]
            else:
                summed[d, q] = part[d, c, q] + from_core[d, q]
                copy(summed.at[d, q], from_y.at[d, y], y_in.at[d], device(dy=dy))

    def after_y(d):
        landed(from_y.at[d, 1:], y_in.at[d])
        chunks[d] = sum(from_y[d, q] for q in range(ny)).reshape(chunks.shape[1:])
        from_zl[d, zl] = chunks[d, zl]
        for dz in range(1, nzl):
            copy(chunks.at[d, lax.rem(zl + dz, nzl)], from_zl.at[d, zl], zl_in.at[d], device(dzl=dz))

    def after_zl(d):
        landed(from_zl.at[d, 1:], zl_in.at[d])
        from_zh[d, zh] = sum(from_zl[d, q] for q in range(nzl))
        for dz in range(1, nzh):
            copy(from_zh.at[d, zh], from_zh.at[d, zh], zh_in.at[d], device(dzh=dz))

    def after_zh(d):
        landed(from_zh.at[d, 1:], zh_in.at[d])
        own[d, zl] = sum(from_zh[d, q] for q in range(nzh))
        for dz in range(1, nzl):
            copy(own.at[d, zl], own.at[d, zl], o_in, device(dzl=dz))

    def weigh(d):
        return lax.dot_general(
            basis[lax.rem(x + d, nx)].reshape(wide, RANK), flat[quarter(d), :],
            (((0,), (0,)), ((), ())), preferred_element_type=F32,
        )

    def relay(d, core, dx):
        for q in range(nzl):
            b = (lax.rem(x + d, nx) * nzl + q) * nc + core
            piece = flat.at[pl.ds(pl.multiple_of(b * rows, rows), rows), :]
            copy(piece, piece, x_in.at[2], device(dx=dx))

    gram(0)
    landed(flat.at[quarter(nx - 1), :], x_in.at[0])
    relay(nx - 1, 0, 1)
    landed(flat.at[quarter(1), :], x_in.at[1])
    relay(1, 1, nx - 1)
    gram(3)
    gram(1)
    inner = weigh(0) + weigh(3) + weigh(1)
    after_core(0)
    after_core(3)
    after_core(1)
    after_y(0)
    if chained:
        pl.semaphore_wait(far_sem, len(step_two))
    landed(flat.at[quarter(2), :], x_in.at[2])

    inner = inner + weigh(2)
    first_image = sum(against(tops, t) for t in thirds(inner)[::-1])
    small[...] = first_image.reshape(small.shape)
    s_in[0] = small[c, y, zl]
    for n, (dy, dz, dc) in enumerate(block_peers):
        src = small.at[lax.rem(c + dc, nc), lax.rem(y + dy, ny), lax.rem(zl + dz, nzl)]
        copy(src, s_in.at[n + 1], si_in, device(dzl=dz, dc=dc, dy=dy))
    gram(2)
    after_y(3)
    after_y(1)
    after_core(2)
    after_zl(0)
    after_y(2)

    landed(s_in.at[1:], si_in)
    place_z = zh * nzl + zl
    s_line[place_z] = jnp.sum(s_in[...], axis=0)
    for d in sorted(line_of, key=lambda d: -min(d, nzl * nzh - d)):
        copy(s_line.at[place_z], s_line.at[place_z], sl_in, along_z(d))
    after_zl(3)
    after_zl(1)
    after_zl(2)
    after_zh(0)

    line = nzl * CHUNK

    def place(dx, dy, core):
        b = (lax.rem(x + dx, nx) * nzl + lax.rem(y + dy, ny)) * nc + core
        return pl.ds(pl.multiple_of(b * line, line), line)

    mine = place(0, 0, c)

    def hops(p):
        return min(p[0], nx - p[0]) + min(p[1], ny - p[1])

    def gather_spread(k):
        src = images.at[k, mine, :]
        for p in sorted(plane, key=lambda p: -hops(p)):
            copy(src, src, p_in.at[k, int(hops(p) > 2)], device(dx=p[0], dy=p[1]))
        copy(src, src, q_in.at[k], device(dc=1))

    def gather_pass(k, far):
        group = [p for p in plane if (hops(p) > 2) == far]
        landed(images.at[k, pl.ds(0, len(group) * line), :], p_in.at[k, int(far)])
        for dx, dy in group:
            src = images.at[k, place(nx - dx, ny - dy, c), :]
            copy(src, src, q_in.at[k], device(dc=1))

    def gather_end(k):
        landed(images.at[k, pl.ds(0, nx * ny * line), :], q_in.at[k])

    def factor(k0, k1):
        lax.fori_loop(k0, k1, lambda b, _: (panel_step(b, work, inverse), 0)[1], 0)

    landed(s_line.at[1:], sl_in)
    images[0, mine, :] = sum(
        s_line[q * nzl : (q + 1) * nzl] for q in range(nzh)
    ).reshape(line, RANK)
    gather_spread(0)
    after_zh(3)
    after_zh(1)
    gather_pass(0, False)
    after_zh(2)
    gather_pass(0, True)
    gather_end(0)
    image[...] = to_unit(images[0])
    landed(own.at[:, 1:], o_in)

    for k in range(1, ITERS):
        images[k, mine, :] = sum(
            jnp.dot(own[d].reshape(line, wide), image[quarter(d), :],
                    preferred_element_type=F32, precision=lax.Precision.HIGHEST)
            for d in range(nx)
        )
        gather_spread(k)
        start_factor(image[...], work)
        factor(0, 5)
        gather_pass(k, False)
        factor(5, RANK // PANEL)
        gather_pass(k, True)
        if k == ITERS - 1:
            waited = len(started) - nx * ny
            for cp in started[:waited]:
                cp.wait_send()
        gather_end(k)
        image[...] = to_unit(lax.dot_general(
            images[k], inverse[...], (((1,), (1,)), ((), ())),
            preferred_element_type=F32, precision=lax.Precision.HIGHEST,
        ))
    start_factor(image[...], work)
    for b in range(RANK // PANEL):
        panel_step(b, work, inverse)
    for cp in started[waited:]:
        cp.wait_send()
    narrow = lax.dot_general(
        image[...], inverse[...], (((1,), (1,)), ((), ())),
        preferred_element_type=F32, precision=lax.Precision.HIGHEST,
    ).astype(BF16)
    out[...] = lax.dot_general(
        narrow, flat[:, pl.ds(pl.multiple_of(x * CELLS, CELLS), CELLS)],
        (((0,), (0,)), ((), ())), preferred_element_type=F32,
    )


def local(grid, slab, start):
    nzl, nx, nc, nzh, ny = (grid[k] for k in ("zl", "x", "c", "zh", "y"))
    rows = slab.shape[0]
    order = start.shape[0]
    wide = order // nx
    deep = nzl * rows // ny
    dma = pltpu.SemaphoreType.DMA
    vmem = pltpu.VMEM
    core = pl.pallas_call(
        functools.partial(kernel, grid),
        out_shape=jax.ShapeDtypeStruct((RANK, CELLS), F32),
        in_specs=[pl.BlockSpec(memory_space=pltpu.HBM)] * 2,
        out_specs=pl.BlockSpec(memory_space=pltpu.VMEM),
        scratch_shapes=[
            vmem((nzl, rows, nx * nc, CELLS), F32),
            vmem((nx, nzl, nc * rows, RANK), BF16),
            vmem((nzl, nc, rows, nx * CELLS), BF16),
            vmem((order, nx * CELLS), BF16),
            vmem((nx, nc, ny, deep, wide), F32),
            vmem((nx, ny, deep, wide), F32),
            vmem((nx, ny, deep, wide), F32),
            vmem((nx, ny, deep, wide), F32),
            vmem((nx, nzl, CHUNK, wide), F32),
            vmem((nx, nzl, CHUNK, wide), F32),
            vmem((nx, nzh, CHUNK, wide), F32),
            vmem((nx, nzl, CHUNK, wide), F32),
            vmem((nc, ny, nzl, CHUNK, RANK), F32),
            vmem((nc * ny * nzl, CHUNK, RANK), F32),
            vmem((nzh * nzl, CHUNK, RANK), F32),
            vmem((order, RANK), F32),
            vmem((ITERS, order, RANK), F32),
            vmem((RANK, 2 * RANK), F32),
            vmem((RANK, RANK), F32),
            dma((nzl + nx + 1,)), dma(()),
            dma((nzl, nc)), dma((3,)), dma((nx,)), dma((nx,)), dma((nx,)), dma((nx,)),
            dma(()), dma(()), dma(()), dma((ITERS, 2)), dma((ITERS,)),
            pltpu.SemaphoreType.REGULAR, pltpu.SemaphoreType.REGULAR,
        ],
        compiler_params=pltpu.CompilerParams(
            collective_id=0, has_side_effects=True, vmem_limit_bytes=55104 * 2**10
        ),
        name="truncate",
    )(slab.reshape(rows, nzl, nx * nc, CELLS), start.reshape(nzl, nx, nc * rows, RANK))
    return core.reshape(RANK, 1, 1, CELLS)


def solution(mesh, grid=GRID):
    placed = (P("fib", "oth", None, None), P())
    return jax.shard_map(
        functools.partial(local, grid), mesh=mesh, in_specs=placed,
        out_specs=P(None, "oth", "fib", None), check_vma=False,
    )
```

```python
import functools

import jax
import jax.numpy as jnp
from jax import lax
from jax.experimental import pallas as pl
from jax.experimental.pallas import tpu as pltpu
from jax.sharding import PartitionSpec as P

ITERS = 3
RANK = 128
CELLS = 128
CHUNK = 8
GRID = dict(zl=4, x=4, c=2, zh=4, y=4)
MESH = pl.DeviceIdType.MESH
F32 = jnp.float32
BF16 = jnp.bfloat16


def thirds(a):
    high = a.astype(BF16)
    rest = a - high.astype(F32)
    mid = rest.astype(BF16)
    return high, mid, (rest - mid.astype(F32)).astype(BF16)


PANEL = 16
TILES = PANEL // 8


def panel_step(b, work, inverse):
    fixed = isinstance(b, int)
    base = b * PANEL if fixed else pl.multiple_of(b * PANEL, PANEL)
    left = work[pl.ds(base, PANEL), 0:RANK]
    right = work[pl.ds(base, PANEL), RANK : 2 * RANK]
    turned, at = (left, base) if fixed else (pltpu.roll(left, RANK - base, 1), 0)
    row = lax.broadcasted_iota(jnp.int32, (8, RANK), 0)
    tiles = []
    for t in range(TILES):
        rows = slice(8 * t, 8 * t + 8)
        cols = [jnp.broadcast_to(turned[rows, at + s : at + s + 1], (8, RANK)) for s in range(PANEL)]
        tiles.append(jnp.stack(cols + [left[rows], right[rows]]))
    pivots = [jnp.ones((8, RANK), F32) for _ in range(TILES)]
    for s in range(PANEL):
        ts, ss = divmod(s, 8)
        pivot = jnp.broadcast_to(tiles[ts][0, ss : ss + 1, :], (8, RANK))
        pivots[ts] = jnp.where(row == ss, pivot, pivots[ts])
        over = 1.0 / pivot
        lead = jnp.broadcast_to(tiles[ts][1:, ss : ss + 1, :], (PANEL + 1 - s, 8, RANK))
        for t in range(TILES):
            rest = tiles[t][1:]
            if t >= ts:
                factor = tiles[t][0] * over
                if t == ts:
                    factor = jnp.where(row > ss, factor, 0.0)
                rest = rest - factor[None] * lead
            tiles[t] = rest
    left = jnp.concatenate([tile[0] for tile in tiles], axis=0)
    right = jnp.concatenate([tile[1] for tile in tiles], axis=0)
    pivots = jnp.concatenate(pivots, axis=0)
    inverse[pl.ds(base, PANEL), :] = right * lax.rsqrt(pivots)
    if fixed and base + PANEL == RANK:
        return
    lane = lax.broadcasted_iota(jnp.int32, (PANEL, RANK), 1)
    factors = jnp.where(lane >= base + PANEL, left * (1.0 / pivots), 0.0)
    fh, fm, fl = thirds(factors)
    rh, rm, rl = thirds(jnp.concatenate([left, right], axis=1))
    tall = jnp.concatenate([fh, fh, fm, fh, fl, fm], axis=0)
    wide = jnp.concatenate([rh, rm, rh, rl, rh, rm], axis=0)
    change = lax.dot_general(tall, wide, (((0,), (0,)), ((), ())), preferred_element_type=F32)
    if fixed:
        work[base + PANEL :, :] = work[base + PANEL :, :] - change[base + PANEL :]
    else:
        work[...] = work[...] - change


def start_factor(image, work):
    work[:, 0:RANK] = lax.dot_general(
        image, image, (((0,), (0,)), ((), ())),
        preferred_element_type=F32, precision=lax.Precision.HIGHEST,
    )
    i0 = lax.broadcasted_iota(jnp.int32, (RANK, RANK), 0)
    i1 = lax.broadcasted_iota(jnp.int32, (RANK, RANK), 1)
    work[:, RANK : 2 * RANK] = (i0 == i1).astype(F32)


def to_unit(image):
    return image * (1.0 / jnp.max(jnp.abs(image)))


def kernel(
    grid, slab, start, out,
    stage, basis, send, flat, part, from_core, summed, from_y, chunks, from_zl, from_zh, own,
    small, s_in, s_line, image, images, work, inverse,
    load_sem, sent, a_in, x_in, c_in, y_in, zl_in, zh_in, o_in, si_in, sl_in, p_in, q_in, near_sem, far_sem,
):
    nzl, nx, nc, nzh, ny = (grid[k] for k in ("zl", "x", "c", "zh", "y"))
    rows = stage.shape[1]
    wide = part.shape[4]
    fib, oth = lax.axis_index("fib"), lax.axis_index("oth")
    c = lax.rem(fib, nc)
    x = lax.rem(lax.div(fib, nc), nx)
    zl = lax.div(fib, nc * nx)
    y = lax.rem(oth, ny)
    zh = lax.div(oth, ny)

    def device(dzl=0, dx=0, dc=0, dzh=0, dy=0):
        f = (lax.rem(zl + dzl, nzl) * nx + lax.rem(x + dx, nx)) * nc + lax.rem(c + dc, nc)
        o = lax.rem(zh + dzh, nzh) * ny + lax.rem(y + dy, ny)
        return (f, o)

    def along_z(d):
        z = lax.rem(zh * nzl + zl + d, nzh * nzl)
        f = (lax.rem(z, nzl) * nx + x) * nc + c
        return (f, lax.div(z, nzl) * ny + y)

    started = []

    def copy(src, dst, rsem, to):
        cp = pltpu.make_async_remote_copy(
            src_ref=src, dst_ref=dst, send_sem=sent, recv_sem=rsem,
            device_id=to, device_id_type=MESH,
        )
        cp.start()
        started.append(cp)
        return cp

    def landed(like, sem):
        pltpu.make_async_copy(like, like, sem).wait()

    run = [(dz, dc) for dz in range(nzl) for dc in range(nc)]
    plane = [(dx, dy) for dx in range(nx) for dy in range(ny) if dx or dy]

    loads = []
    for dz in range(nzl):
        to_zl = lax.rem(zl + dz, nzl)
        load = pltpu.make_async_copy(slab.at[:, to_zl], stage.at[dz], load_sem.at[dz])
        load.start()
        loads.append(load)
    barrier = pltpu.get_barrier_semaphore()
    block_peers = [
        (dy, dz, dc) for dy in range(ny) for dz in range(nzl) for dc in range(nc) if dy or dz or dc
    ]
    line_of = range(1, nzl * nzh)
    chained = nzl == 4 and nzh == 4
    peers = [device(dzl=dz, dc=dc, dy=dy) for dy, dz, dc in block_peers if dy == 0 or not chained]
    peers += [device(dx=dx) for dx in range(1, nx)]
    if chained:
        step_one = [along_z(2), along_z(14), device(dy=1), device(dy=ny - 1)]
        step_two = [along_z(4), along_z(12), device(dy=1), device(dy=ny - 1)]
        peers += step_one
    else:
        peers += [along_z(d) for d in line_of]
    for peer in peers:
        pl.semaphore_signal(barrier, inc=1, device_id=peer, device_id_type=MESH)

    for k in range(nx):
        load = pltpu.make_async_copy(start.at[:, k], basis.at[k], load_sem.at[nzl + k])
        load.start()
        loads.append(load)

    def block(dx, dz, dc):
        b = (lax.rem(x + dx, nx) * nzl + lax.rem(zl + nzl - dz, nzl)) * nc + lax.rem(c + nc - dc, nc)
        return flat.at[pl.ds(pl.multiple_of(b * rows, rows), rows), :]

    def quarter(dx):
        return pl.ds(pl.multiple_of(lax.rem(x + dx, nx) * wide, wide), wide)

    here = block(0, 0, 0)
    keep = pltpu.make_async_copy(send.at[0, 0], here, load_sem.at[nzl + nx])
    for dz in range(nzl):
        loads[dz].wait()
        for px in range(nx):
            v0 = stage[dz, :, px * nc, :]
            v1 = stage[dz, :, px * nc + 1, :]
            send[dz, 0, :, px * CELLS : (px + 1) * CELLS] = jnp.where(c == 0, v0, v1).astype(BF16)
            send[dz, 1, :, px * CELLS : (px + 1) * CELLS] = jnp.where(c == 0, v1, v0).astype(BF16)
        if dz == 0:
            keep.start()
            pl.semaphore_wait(barrier, len(peers))
            if chained:
                for peer in step_one:
                    pl.semaphore_signal(near_sem, inc=1, device_id=peer, device_id_type=MESH)
        for dc in range(nc):
            if dz or dc:
                copy(send.at[dz, dc], here, a_in.at[dz, dc], device(dzl=dz, dc=dc))
        if dz == 0:
            copy(send.at[0, 0], here, x_in.at[0], device(dx=1))
            copy(send.at[0, 0], here, x_in.at[1], device(dx=nx - 1))
    for p in run[1:]:
        piece = block(0, *p)
        landed(piece, a_in.at[p])
        copy(piece, piece, x_in.at[0], device(dx=1))
        copy(piece, piece, x_in.at[1], device(dx=nx - 1))
    if chained:
        pl.semaphore_wait(near_sem, len(step_one))
        for peer in step_two:
            pl.semaphore_signal(far_sem, inc=1, device_id=peer, device_id_type=MESH)
    keep.wait()
    for load in loads[nzl:]:
        load.wait()

    def against(a, b):
        return lax.dot_general(a, b, (((1,), (1,)), ((), ())), preferred_element_type=F32)

    tops = jnp.concatenate([
        flat[pl.ds(pl.multiple_of(((x * nzl + q) * nc + k) * rows, rows), rows), :]
        for k in range(nc) for q in range(nzl)
    ], axis=0)

    def gram(d):
        part[d] = against(tops, flat[quarter(d), :]).reshape(part.shape[1:])
        copy(part.at[d, 1 - c], from_core.at[d], c_in.at[d], device(dc=1))

    def after_core(d):
        landed(from_core.at[d], c_in.at[d])
        for dy in (2, 1, 3, 0):
            q = lax.rem(y + dy, ny)
            if dy == 0:
                from_y[d, y] = part[d, c, q] + from_core[d, q]
            else:
                summed[d, q] = part[d, c, q] + from_core[d, q]
                copy(summed.at[d, q], from_y.at[d, y], y_in.at[d], device(dy=dy))

    def after_y(d):
        landed(from_y.at[d, 1:], y_in.at[d])
        chunks[d] = sum(from_y[d, q] for q in range(ny)).reshape(chunks.shape[1:])
        from_zl[d, zl] = chunks[d, zl]
        for dz in range(1, nzl):
            copy(chunks.at[d, lax.rem(zl + dz, nzl)], from_zl.at[d, zl], zl_in.at[d], device(dzl=dz))

    def after_zl(d):
        landed(from_zl.at[d, 1:], zl_in.at[d])
        from_zh[d, zh] = sum(from_zl[d, q] for q in range(nzl))
        for dz in range(1, nzh):
            copy(from_zh.at[d, zh], from_zh.at[d, zh], zh_in.at[d], device(dzh=dz))

    def after_zh(d):
        landed(from_zh.at[d, 1:], zh_in.at[d])
        own[d, zl] = sum(from_zh[d, q] for q in range(nzh))
        for dz in range(1, nzl):
            copy(own.at[d, zl], own.at[d, zl], o_in, device(dzl=dz))

    def weigh(d):
        return lax.dot_general(
            basis[lax.rem(x + d, nx)].reshape(wide, RANK), flat[quarter(d), :],
            (((0,), (0,)), ((), ())), preferred_element_type=F32,
        )

    def relay(d, core, dx):
        for q in range(nzl):
            b = (lax.rem(x + d, nx) * nzl + q) * nc + core
            piece = flat.at[pl.ds(pl.multiple_of(b * rows, rows), rows), :]
            copy(piece, piece, x_in.at[2], device(dx=dx))

    gram(0)
    landed(flat.at[quarter(nx - 1), :], x_in.at[0])
    relay(nx - 1, 0, 1)
    landed(flat.at[quarter(1), :], x_in.at[1])
    relay(1, 1, nx - 1)
    gram(3)
    gram(1)
    inner = weigh(0) + weigh(3) + weigh(1)
    after_core(0)
    after_core(3)
    after_core(1)
    after_y(0)
    if chained:
        pl.semaphore_wait(far_sem, len(step_two))
    landed(flat.at[quarter(2), :], x_in.at[2])

    inner = inner + weigh(2)
    first_image = sum(against(tops, t) for t in thirds(inner)[::-1])
    small[...] = first_image.reshape(small.shape)
    s_in[0] = small[c, y, zl]
    reach = lambda p: min(p[0], ny - p[0]) + min(p[1], nzl - p[1])
    for n, (dy, dz, dc) in sorted(enumerate(block_peers), key=lambda p: -reach(p[1])):
        src = small.at[lax.rem(c + dc, nc), lax.rem(y + dy, ny), lax.rem(zl + dz, nzl)]
        copy(src, s_in.at[n + 1], si_in, device(dzl=dz, dc=dc, dy=dy))
    gram(2)
    after_y(3)
    after_y(1)
    after_core(2)
    after_zl(0)
    after_y(2)

    landed(s_in.at[1:], si_in)
    place_z = zh * nzl + zl
    s_line[place_z] = jnp.sum(s_in[...], axis=0)
    for d in sorted(line_of, key=lambda d: -min(d, nzl * nzh - d)):
        copy(s_line.at[place_z], s_line.at[place_z], sl_in, along_z(d))
    after_zl(3)
    after_zl(1)
    after_zl(2)

    line = nzl * CHUNK

    def place(dx, dy, core):
        b = (lax.rem(x + dx, nx) * nzl + lax.rem(y + dy, ny)) * nc + core
        return pl.ds(pl.multiple_of(b * line, line), line)

    mine = place(0, 0, c)

    def hops(p):
        return min(p[0], nx - p[0]) + min(p[1], ny - p[1])

    def gather_spread(k):
        src = images.at[k, mine, :]
        for p in sorted(plane, key=lambda p: -hops(p)):
            copy(src, src, p_in.at[k, int(hops(p) > 2)], device(dx=p[0], dy=p[1]))
        copy(src, src, q_in.at[k], device(dc=1))

    def gather_pass(k, far):
        group = [p for p in plane if (hops(p) > 2) == far]
        landed(images.at[k, pl.ds(0, len(group) * line), :], p_in.at[k, int(far)])
        for dx, dy in group:
            src = images.at[k, place(nx - dx, ny - dy, c), :]
            copy(src, src, q_in.at[k], device(dc=1))

    def gather_end(k):
        landed(images.at[k, pl.ds(0, nx * ny * line), :], q_in.at[k])

    def factor(k0, k1):
        lax.fori_loop(k0, k1, lambda b, _: (panel_step(b, work, inverse), 0)[1], 0)

    landed(s_line.at[1:], sl_in)
    images[0, mine, :] = sum(
        s_line[q * nzl : (q + 1) * nzl] for q in range(nzh)
    ).reshape(line, RANK)
    gather_spread(0)
    after_zh(0)
    after_zh(3)
    after_zh(1)
    gather_pass(0, False)
    after_zh(2)
    gather_pass(0, True)
    gather_end(0)
    image[...] = to_unit(images[0])

    def times(strip, d):
        return jnp.dot(strip, image[quarter(d), :], preferred_element_type=F32, precision=lax.Precision.HIGHEST)

    landed(own.at[:, 1:], o_in)
    for k in range(1, ITERS):
        images[k, mine, :] = sum(times(own[d].reshape(line, wide), d) for d in range(nx))
        gather_spread(k)
        start_factor(image[...], work)
        factor(0, 5)
        gather_pass(k, False)
        factor(5, RANK // PANEL)
        gather_pass(k, True)
        gather_end(k)
        image[...] = to_unit(lax.dot_general(
            images[k], inverse[...], (((1,), (1,)), ((), ())),
            preferred_element_type=F32, precision=lax.Precision.HIGHEST,
        ))
    start_factor(image[...], work)
    for b in range(RANK // PANEL):
        panel_step(b, work, inverse)
    for cp in started:
        cp.wait_send()
    narrow = lax.dot_general(
        image[...], inverse[...], (((1,), (1,)), ((), ())),
        preferred_element_type=F32, precision=lax.Precision.HIGHEST,
    ).astype(BF16)
    out[...] = lax.dot_general(
        narrow, flat[:, pl.ds(pl.multiple_of(x * CELLS, CELLS), CELLS)],
        (((0,), (0,)), ((), ())), preferred_element_type=F32,
    )


def local(grid, slab, start):
    nzl, nx, nc, nzh, ny = (grid[k] for k in ("zl", "x", "c", "zh", "y"))
    rows = slab.shape[0]
    order = start.shape[0]
    wide = order // nx
    deep = nzl * rows // ny
    dma = pltpu.SemaphoreType.DMA
    vmem = pltpu.VMEM
    core = pl.pallas_call(
        functools.partial(kernel, grid),
        out_shape=jax.ShapeDtypeStruct((RANK, CELLS), F32),
        in_specs=[pl.BlockSpec(memory_space=pltpu.HBM)] * 2,
        out_specs=pl.BlockSpec(memory_space=pltpu.VMEM),
        scratch_shapes=[
            vmem((nzl, rows, nx * nc, CELLS), F32),
            vmem((nx, nzl, nc * rows, RANK), BF16),
            vmem((nzl, nc, rows, nx * CELLS), BF16),
            vmem((order, nx * CELLS), BF16),
            vmem((nx, nc, ny, deep, wide), F32),
            vmem((nx, ny, deep, wide), F32),
            vmem((nx, ny, deep, wide), F32),
            vmem((nx, ny, deep, wide), F32),
            vmem((nx, nzl, CHUNK, wide), F32),
            vmem((nx, nzl, CHUNK, wide), F32),
            vmem((nx, nzh, CHUNK, wide), F32),
            vmem((nx, nzl, CHUNK, wide), F32),
            vmem((nc, ny, nzl, CHUNK, RANK), F32),
            vmem((nc * ny * nzl, CHUNK, RANK), F32),
            vmem((nzh * nzl, CHUNK, RANK), F32),
            vmem((order, RANK), F32),
            vmem((ITERS, order, RANK), F32),
            vmem((RANK, 2 * RANK), F32),
            vmem((RANK, RANK), F32),
            dma((nzl + nx + 1,)), dma(()),
            dma((nzl, nc)), dma((3,)), dma((nx,)), dma((nx,)), dma((nx,)), dma((nx,)),
            dma(()), dma(()), dma(()), dma((ITERS, 2)), dma((ITERS,)),
            pltpu.SemaphoreType.REGULAR, pltpu.SemaphoreType.REGULAR,
        ],
        compiler_params=pltpu.CompilerParams(
            collective_id=0, has_side_effects=True, vmem_limit_bytes=55104 * 2**10
        ),
        name="truncate",
    )(slab.reshape(rows, nzl, nx * nc, CELLS), start.reshape(nzl, nx, nc * rows, RANK))
    return core.reshape(RANK, 1, 1, CELLS)


def solution(mesh, grid=GRID):
    placed = (P("fib", "oth", None, None), P())
    return jax.shard_map(
        functools.partial(local, grid), mesh=mesh, in_specs=placed,
        out_specs=P(None, "oth", "fib", None), check_vma=False,
    )
```

```python
import functools

import jax
import jax.numpy as jnp
from jax import lax
from jax.experimental import pallas as pl
from jax.experimental.pallas import tpu as pltpu
from jax.sharding import PartitionSpec as P

ITERS = 3
RANK = 128
CELLS = 128
CHUNK = 8
GRID = dict(zl=4, x=4, c=2, zh=4, y=4)
MESH = pl.DeviceIdType.MESH
F32 = jnp.float32
BF16 = jnp.bfloat16


def thirds(a):
    high = a.astype(BF16)
    rest = a - high.astype(F32)
    mid = rest.astype(BF16)
    return high, mid, (rest - mid.astype(F32)).astype(BF16)


PANEL = 16
TILES = PANEL // 8


def panel_step(b, work, inverse):
    fixed = isinstance(b, int)
    base = b * PANEL if fixed else pl.multiple_of(b * PANEL, PANEL)
    left = work[pl.ds(base, PANEL), 0:RANK]
    right = work[pl.ds(base, PANEL), RANK : 2 * RANK]
    turned, at = (left, base) if fixed else (pltpu.roll(left, RANK - base, 1), 0)
    row = lax.broadcasted_iota(jnp.int32, (8, RANK), 0)
    tiles = []
    for t in range(TILES):
        rows = slice(8 * t, 8 * t + 8)
        cols = [jnp.broadcast_to(turned[rows, at + s : at + s + 1], (8, RANK)) for s in range(PANEL)]
        tiles.append(jnp.stack(cols + [left[rows], right[rows]]))
    pivots = [jnp.ones((8, RANK), F32) for _ in range(TILES)]
    for s in range(PANEL):
        ts, ss = divmod(s, 8)
        pivot = jnp.broadcast_to(tiles[ts][0, ss : ss + 1, :], (8, RANK))
        pivots[ts] = jnp.where(row == ss, pivot, pivots[ts])
        over = 1.0 / pivot
        lead = jnp.broadcast_to(tiles[ts][1:, ss : ss + 1, :], (PANEL + 1 - s, 8, RANK))
        for t in range(TILES):
            rest = tiles[t][1:]
            if t >= ts:
                factor = tiles[t][0] * over
                if t == ts:
                    factor = jnp.where(row > ss, factor, 0.0)
                rest = rest - factor[None] * lead
            tiles[t] = rest
    left = jnp.concatenate([tile[0] for tile in tiles], axis=0)
    right = jnp.concatenate([tile[1] for tile in tiles], axis=0)
    pivots = jnp.concatenate(pivots, axis=0)
    inverse[pl.ds(base, PANEL), :] = right * lax.rsqrt(pivots)
    if fixed and base + PANEL == RANK:
        return
    lane = lax.broadcasted_iota(jnp.int32, (PANEL, RANK), 1)
    factors = jnp.where(lane >= base + PANEL, left * (1.0 / pivots), 0.0)
    fh, fm, fl = thirds(factors)
    rh, rm, rl = thirds(jnp.concatenate([left, right], axis=1))
    tall = jnp.concatenate([fh, fh, fm, fh, fl, fm], axis=0)
    wide = jnp.concatenate([rh, rm, rh, rl, rh, rm], axis=0)
    change = lax.dot_general(tall, wide, (((0,), (0,)), ((), ())), preferred_element_type=F32)
    if fixed:
        work[base + PANEL :, :] = work[base + PANEL :, :] - change[base + PANEL :]
    else:
        work[...] = work[...] - change


def start_factor(image, work):
    work[:, 0:RANK] = lax.dot_general(
        image, image, (((0,), (0,)), ((), ())),
        preferred_element_type=F32, precision=lax.Precision.HIGHEST,
    )
    i0 = lax.broadcasted_iota(jnp.int32, (RANK, RANK), 0)
    i1 = lax.broadcasted_iota(jnp.int32, (RANK, RANK), 1)
    work[:, RANK : 2 * RANK] = (i0 == i1).astype(F32)


def to_unit(image):
    return image * (1.0 / jnp.max(jnp.abs(image)))


def kernel(
    grid, slab, start, out,
    stage, basis, send, flat, part, from_core, summed, from_y, chunks, from_zl, from_zh, own,
    small, s_in, s_line, image, images, work, inverse,
    load_sem, sent, a_in, x_in, c_in, y_in, zl_in, zh_in, o_in, si_in, sl_in, p_in, q_in, near_sem, far_sem,
):
    nzl, nx, nc, nzh, ny = (grid[k] for k in ("zl", "x", "c", "zh", "y"))
    rows = stage.shape[1]
    wide = part.shape[4]
    fib, oth = lax.axis_index("fib"), lax.axis_index("oth")
    c = lax.rem(fib, nc)
    x = lax.rem(lax.div(fib, nc), nx)
    zl = lax.div(fib, nc * nx)
    y = lax.rem(oth, ny)
    zh = lax.div(oth, ny)

    def device(dzl=0, dx=0, dc=0, dzh=0, dy=0):
        f = (lax.rem(zl + dzl, nzl) * nx + lax.rem(x + dx, nx)) * nc + lax.rem(c + dc, nc)
        o = lax.rem(zh + dzh, nzh) * ny + lax.rem(y + dy, ny)
        return (f, o)

    def along_z(d):
        z = lax.rem(zh * nzl + zl + d, nzh * nzl)
        f = (lax.rem(z, nzl) * nx + x) * nc + c
        return (f, lax.div(z, nzl) * ny + y)

    started = []

    def copy(src, dst, rsem, to):
        cp = pltpu.make_async_remote_copy(
            src_ref=src, dst_ref=dst, send_sem=sent, recv_sem=rsem,
            device_id=to, device_id_type=MESH,
        )
        cp.start()
        started.append(cp)
        return cp

    def landed(like, sem):
        pltpu.make_async_copy(like, like, sem).wait()

    run = [(dz, dc) for dz in range(nzl) for dc in range(nc)]
    plane = [(dx, dy) for dx in range(nx) for dy in range(ny) if dx or dy]

    loads = []
    for dz in range(nzl):
        to_zl = lax.rem(zl + dz, nzl)
        load = pltpu.make_async_copy(slab.at[:, to_zl], stage.at[dz], load_sem.at[dz])
        load.start()
        loads.append(load)
    barrier = pltpu.get_barrier_semaphore()
    block_peers = [
        (dy, dz, dc) for dy in range(ny) for dz in range(nzl) for dc in range(nc) if dy or dz or dc
    ]
    line_of = range(1, nzl * nzh)
    chained = nzl == 4 and nzh == 4
    peers = [device(dzl=dz, dc=dc, dy=dy) for dy, dz, dc in block_peers if dy == 0 or not chained]
    peers += [device(dx=dx) for dx in range(1, nx)]
    if chained:
        step_one = [along_z(2), along_z(14), device(dy=1), device(dy=ny - 1)]
        step_two = [along_z(4), along_z(12), device(dy=1), device(dy=ny - 1)]
        peers += step_one
    else:
        peers += [along_z(d) for d in line_of]
    for peer in peers:
        pl.semaphore_signal(barrier, inc=1, device_id=peer, device_id_type=MESH)

    for k in range(nx):
        load = pltpu.make_async_copy(start.at[:, k], basis.at[k], load_sem.at[nzl + k])
        load.start()
        loads.append(load)

    def block(dx, dz, dc):
        b = (lax.rem(x + dx, nx) * nzl + lax.rem(zl + nzl - dz, nzl)) * nc + lax.rem(c + nc - dc, nc)
        return flat.at[pl.ds(pl.multiple_of(b * rows, rows), rows), :]

    def quarter(dx):
        return pl.ds(pl.multiple_of(lax.rem(x + dx, nx) * wide, wide), wide)

    here = block(0, 0, 0)
    keep = pltpu.make_async_copy(send.at[0, 0], here, load_sem.at[nzl + nx])
    for dz in range(nzl):
        loads[dz].wait()
        for px in range(nx):
            v0 = stage[dz, :, px * nc, :]
            v1 = stage[dz, :, px * nc + 1, :]
            send[dz, 0, :, px * CELLS : (px + 1) * CELLS] = jnp.where(c == 0, v0, v1).astype(BF16)
            send[dz, 1, :, px * CELLS : (px + 1) * CELLS] = jnp.where(c == 0, v1, v0).astype(BF16)
        if dz == 0:
            keep.start()
            pl.semaphore_wait(barrier, len(peers))
            if chained:
                for peer in step_one:
                    pl.semaphore_signal(near_sem, inc=1, device_id=peer, device_id_type=MESH)
        for dc in range(nc):
            if dz or dc:
                copy(send.at[dz, dc], here, a_in.at[dz, dc], device(dzl=dz, dc=dc))
        if dz == 0:
            copy(send.at[0, 0], here, x_in.at[0], device(dx=1))
            copy(send.at[0, 0], here, x_in.at[1], device(dx=nx - 1))
    for p in run[1:]:
        piece = block(0, *p)
        landed(piece, a_in.at[p])
        copy(piece, piece, x_in.at[0], device(dx=1))
        copy(piece, piece, x_in.at[1], device(dx=nx - 1))
    if chained:
        pl.semaphore_wait(near_sem, len(step_one))
        for peer in step_two:
            pl.semaphore_signal(far_sem, inc=1, device_id=peer, device_id_type=MESH)
    keep.wait()
    for load in loads[nzl:]:
        load.wait()

    def against(a, b):
        return lax.dot_general(a, b, (((1,), (1,)), ((), ())), preferred_element_type=F32)

    tops = jnp.concatenate([
        flat[pl.ds(pl.multiple_of(((x * nzl + q) * nc + k) * rows, rows), rows), :]
        for k in range(nc) for q in range(nzl)
    ], axis=0)

    def gram(d):
        part[d] = against(tops, flat[quarter(d), :]).reshape(part.shape[1:])
        copy(part.at[d, 1 - c], from_core.at[d], c_in.at[d], device(dc=1))

    def after_core(d):
        landed(from_core.at[d], c_in.at[d])
        for dy in (2, 1, 3, 0):
            q = lax.rem(y + dy, ny)
            if dy == 0:
                from_y[d, y] = part[d, c, q] + from_core[d, q]
            else:
                summed[d, q] = part[d, c, q] + from_core[d, q]
                copy(summed.at[d, q], from_y.at[d, y], y_in.at[d], device(dy=dy))

    def after_y(d):
        landed(from_y.at[d, 1:], y_in.at[d])
        chunks[d] = sum(from_y[d, q] for q in range(ny)).reshape(chunks.shape[1:])
        from_zl[d, zl] = chunks[d, zl]
        for dz in range(1, nzl):
            copy(chunks.at[d, lax.rem(zl + dz, nzl)], from_zl.at[d, zl], zl_in.at[d], device(dzl=dz))

    def after_zl(d):
        landed(from_zl.at[d, 1:], zl_in.at[d])
        from_zh[d, zh] = sum(from_zl[d, q] for q in range(nzl))
        for dz in range(1, nzh):
            copy(from_zh.at[d, zh], from_zh.at[d, zh], zh_in.at[d], device(dzh=dz))

    def after_zh(d):
        landed(from_zh.at[d, 1:], zh_in.at[d])
        own[d, zl] = sum(from_zh[d, q] for q in range(nzh))
        for dz in range(1, nzl):
            copy(own.at[d, zl], own.at[d, zl], o_in, device(dzl=dz))

    def weigh(d):
        return lax.dot_general(
            basis[lax.rem(x + d, nx)].reshape(wide, RANK), flat[quarter(d), :],
            (((0,), (0,)), ((), ())), preferred_element_type=F32,
        )

    def relay(d, core, dx):
        for q in range(nzl):
            b = (lax.rem(x + d, nx) * nzl + q) * nc + core
            piece = flat.at[pl.ds(pl.multiple_of(b * rows, rows), rows), :]
            copy(piece, piece, x_in.at[2], device(dx=dx))

    gram(0)
    landed(flat.at[quarter(nx - 1), :], x_in.at[0])
    relay(nx - 1, 0, 1)
    landed(flat.at[quarter(1), :], x_in.at[1])
    relay(1, 1, nx - 1)
    gram(3)
    gram(1)
    inner = weigh(0) + weigh(3) + weigh(1)
    after_core(0)
    after_core(3)
    after_core(1)
    if chained:
        pl.semaphore_wait(far_sem, len(step_two))
    landed(flat.at[quarter(2), :], x_in.at[2])

    inner = inner + weigh(2)
    first_image = sum(against(tops, t) for t in thirds(inner)[::-1])
    small[...] = first_image.reshape(small.shape)
    s_in[0] = small[c, y, zl]
    reach = lambda p: min(p[0], ny - p[0]) + min(p[1], nzl - p[1])
    for n, (dy, dz, dc) in sorted(enumerate(block_peers), key=lambda p: -reach(p[1])):
        src = small.at[lax.rem(c + dc, nc), lax.rem(y + dy, ny), lax.rem(zl + dz, nzl)]
        copy(src, s_in.at[n + 1], si_in, device(dzl=dz, dc=dc, dy=dy))
    gram(2)
    after_y(0)
    after_y(3)
    after_y(1)
    after_core(2)
    after_zl(0)
    after_y(2)

    landed(s_in.at[1:], si_in)
    place_z = zh * nzl + zl
    s_line[place_z] = jnp.sum(s_in[...], axis=0)
    for d in sorted(line_of, key=lambda d: -min(d, nzl * nzh - d)):
        copy(s_line.at[place_z], s_line.at[place_z], sl_in, along_z(d))
    after_zl(3)
    after_zl(1)
    after_zl(2)

    line = nzl * CHUNK

    def hops(p):
        return min(p[0], nx - p[0]) + min(p[1], ny - p[1])

    def group_of(p):
        return min(p[0], nx - p[0])

    def gather_spread(k):
        src = images.at[k, x, y, c]
        for p in sorted(plane, key=lambda p: (-group_of(p), -hops(p))):
            copy(src, src, p_in.at[k, group_of(p)], device(dx=p[0], dy=p[1]))

    def gather_pass(k, group):
        like = (images.at[k, 0, 1:, 0], images.at[k, 0:2, :, 0], images.at[k, 0, :, 0])[group]
        landed(like, p_in.at[k, group])
        for dx in range(nx):
            if group_of((dx, 0)) == group:
                src = images.at[k, lax.rem(x + dx, nx), :, c]
                copy(src, src, q_in.at[k], device(dc=1))

    def gather_end(k):
        landed(images.at[k, :, :, 0], q_in.at[k])

    def factor(k0, k1):
        lax.fori_loop(k0, k1, lambda b, _: (panel_step(b, work, inverse), 0)[1], 0)

    landed(s_line.at[1:], sl_in)
    images[0, x, y, c] = sum(
        s_line[q * nzl : (q + 1) * nzl] for q in range(nzh)
    ).reshape(line, RANK)
    gather_spread(0)
    after_zh(0)
    after_zh(3)
    after_zh(1)
    gather_pass(0, 0)
    gather_pass(0, 1)
    after_zh(2)
    gather_pass(0, 2)
    gather_end(0)
    image[...] = to_unit(images[0].reshape(image.shape))

    def times(strip, d):
        return jnp.dot(strip, image[quarter(d), :], preferred_element_type=F32, precision=lax.Precision.HIGHEST)

    landed(own.at[:, 1:], o_in)
    for k in range(1, ITERS):
        images[k, x, y, c] = sum(times(own[d].reshape(line, wide), d) for d in range(nx))
        gather_spread(k)
        start_factor(image[...], work)
        factor(0, 5)
        gather_pass(k, 0)
        gather_pass(k, 1)
        factor(5, RANK // PANEL)
        gather_pass(k, 2)
        gather_end(k)
        image[...] = to_unit(lax.dot_general(
            images[k].reshape(image.shape), inverse[...], (((1,), (1,)), ((), ())),
            preferred_element_type=F32, precision=lax.Precision.HIGHEST,
        ))
    start_factor(image[...], work)
    for b in range(RANK // PANEL):
        panel_step(b, work, inverse)
    for cp in started:
        cp.wait_send()
    narrow = lax.dot_general(
        image[...], inverse[...], (((1,), (1,)), ((), ())),
        preferred_element_type=F32, precision=lax.Precision.HIGHEST,
    ).astype(BF16)
    out[...] = lax.dot_general(
        narrow, flat[:, pl.ds(pl.multiple_of(x * CELLS, CELLS), CELLS)],
        (((0,), (0,)), ((), ())), preferred_element_type=F32,
    )


def local(grid, slab, start):
    nzl, nx, nc, nzh, ny = (grid[k] for k in ("zl", "x", "c", "zh", "y"))
    rows = slab.shape[0]
    order = start.shape[0]
    wide = order // nx
    deep = nzl * rows // ny
    dma = pltpu.SemaphoreType.DMA
    vmem = pltpu.VMEM
    core = pl.pallas_call(
        functools.partial(kernel, grid),
        out_shape=jax.ShapeDtypeStruct((RANK, CELLS), F32),
        in_specs=[pl.BlockSpec(memory_space=pltpu.HBM)] * 2,
        out_specs=pl.BlockSpec(memory_space=pltpu.VMEM),
        scratch_shapes=[
            vmem((nzl, rows, nx * nc, CELLS), F32),
            vmem((nx, nzl, nc * rows, RANK), BF16),
            vmem((nzl, nc, rows, nx * CELLS), BF16),
            vmem((order, nx * CELLS), BF16),
            vmem((nx, nc, ny, deep, wide), F32),
            vmem((nx, ny, deep, wide), F32),
            vmem((nx, ny, deep, wide), F32),
            vmem((nx, ny, deep, wide), F32),
            vmem((nx, nzl, CHUNK, wide), F32),
            vmem((nx, nzl, CHUNK, wide), F32),
            vmem((nx, nzh, CHUNK, wide), F32),
            vmem((nx, nzl, CHUNK, wide), F32),
            vmem((nc, ny, nzl, CHUNK, RANK), F32),
            vmem((nc * ny * nzl, CHUNK, RANK), F32),
            vmem((nzh * nzl, CHUNK, RANK), F32),
            vmem((order, RANK), F32),
            vmem((ITERS, nx, ny, nc, nzl * CHUNK, RANK), F32),
            vmem((RANK, 2 * RANK), F32),
            vmem((RANK, RANK), F32),
            dma((nzl + nx + 1,)), dma(()),
            dma((nzl, nc)), dma((3,)), dma((nx,)), dma((nx,)), dma((nx,)), dma((nx,)),
            dma(()), dma(()), dma(()), dma((ITERS, 3)), dma((ITERS,)),
            pltpu.SemaphoreType.REGULAR, pltpu.SemaphoreType.REGULAR,
        ],
        compiler_params=pltpu.CompilerParams(
            collective_id=0, has_side_effects=True, vmem_limit_bytes=55104 * 2**10
        ),
        name="truncate",
    )(slab.reshape(rows, nzl, nx * nc, CELLS), start.reshape(nzl, nx, nc * rows, RANK))
    return core.reshape(RANK, 1, 1, CELLS)


def solution(mesh, grid=GRID):
    placed = (P("fib", "oth", None, None), P())
    return jax.shard_map(
        functools.partial(local, grid), mesh=mesh, in_specs=placed,
        out_specs=P(None, "oth", "fib", None), check_vma=False,
    )
```

```python
import functools

import jax
import jax.numpy as jnp
from jax import lax
from jax.experimental import pallas as pl
from jax.experimental.pallas import tpu as pltpu
from jax.sharding import PartitionSpec as P

ITERS = 3
RANK = 128
CELLS = 128
CHUNK = 8
GRID = dict(zl=4, x=4, c=2, zh=4, y=4)
MESH = pl.DeviceIdType.MESH
F32 = jnp.float32
BF16 = jnp.bfloat16


def thirds(a):
    high = a.astype(BF16)
    rest = a - high.astype(F32)
    mid = rest.astype(BF16)
    return high, mid, (rest - mid.astype(F32)).astype(BF16)


PANEL = 16
TILES = PANEL // 8


def panel_step(b, work, inverse):
    fixed = isinstance(b, int)
    base = b * PANEL if fixed else pl.multiple_of(b * PANEL, PANEL)
    left = work[pl.ds(base, PANEL), 0:RANK]
    right = work[pl.ds(base, PANEL), RANK : 2 * RANK]
    turned, at = (left, base) if fixed else (pltpu.roll(left, RANK - base, 1), 0)
    row = lax.broadcasted_iota(jnp.int32, (8, RANK), 0)
    tiles = []
    for t in range(TILES):
        rows = slice(8 * t, 8 * t + 8)
        cols = [jnp.broadcast_to(turned[rows, at + s : at + s + 1], (8, RANK)) for s in range(PANEL)]
        tiles.append(jnp.stack(cols + [left[rows], right[rows]]))
    pivots = [jnp.ones((8, RANK), F32) for _ in range(TILES)]
    for s in range(PANEL):
        ts, ss = divmod(s, 8)
        pivot = jnp.broadcast_to(tiles[ts][0, ss : ss + 1, :], (8, RANK))
        pivots[ts] = jnp.where(row == ss, pivot, pivots[ts])
        over = 1.0 / pivot
        lead = jnp.broadcast_to(tiles[ts][1:, ss : ss + 1, :], (PANEL + 1 - s, 8, RANK))
        for t in range(TILES):
            rest = tiles[t][1:]
            if t >= ts:
                factor = tiles[t][0] * over
                if t == ts:
                    factor = jnp.where(row > ss, factor, 0.0)
                rest = rest - factor[None] * lead
            tiles[t] = rest
    left = jnp.concatenate([tile[0] for tile in tiles], axis=0)
    right = jnp.concatenate([tile[1] for tile in tiles], axis=0)
    pivots = jnp.concatenate(pivots, axis=0)
    inverse[pl.ds(base, PANEL), :] = right * lax.rsqrt(pivots)
    if fixed and base + PANEL == RANK:
        return
    lane = lax.broadcasted_iota(jnp.int32, (PANEL, RANK), 1)
    factors = jnp.where(lane >= base + PANEL, left * (1.0 / pivots), 0.0)
    fh, fm, fl = thirds(factors)
    rh, rm, rl = thirds(jnp.concatenate([left, right], axis=1))
    tall = jnp.concatenate([fh, fh, fm, fh, fl, fm], axis=0)
    wide = jnp.concatenate([rh, rm, rh, rl, rh, rm], axis=0)
    change = lax.dot_general(tall, wide, (((0,), (0,)), ((), ())), preferred_element_type=F32)
    if fixed:
        work[base + PANEL :, :] = work[base + PANEL :, :] - change[base + PANEL :]
    else:
        work[...] = work[...] - change


def start_factor(image, work):
    work[:, 0:RANK] = lax.dot_general(
        image, image, (((0,), (0,)), ((), ())),
        preferred_element_type=F32, precision=lax.Precision.HIGHEST,
    )
    i0 = lax.broadcasted_iota(jnp.int32, (RANK, RANK), 0)
    i1 = lax.broadcasted_iota(jnp.int32, (RANK, RANK), 1)
    work[:, RANK : 2 * RANK] = (i0 == i1).astype(F32)


def to_unit(image):
    return image * (1.0 / jnp.max(jnp.abs(image)))


def kernel(
    grid, slab, start, out,
    stage, basis, send, flat, part, from_core, summed, from_y, chunks, from_zl, from_zh, own,
    small, s_in, s_line, image, images, work, inverse,
    load_sem, sent, a_in, x_in, c_in, y_in, zl_in, zh_in, o_in, si_in, sl_in, p_in, q_in, near_sem, far_sem,
):
    nzl, nx, nc, nzh, ny = (grid[k] for k in ("zl", "x", "c", "zh", "y"))
    rows = stage.shape[1]
    wide = part.shape[4]
    fib, oth = lax.axis_index("fib"), lax.axis_index("oth")
    c = lax.rem(fib, nc)
    x = lax.rem(lax.div(fib, nc), nx)
    zl = lax.div(fib, nc * nx)
    y = lax.rem(oth, ny)
    zh = lax.div(oth, ny)

    def device(dzl=0, dx=0, dc=0, dzh=0, dy=0):
        f = (lax.rem(zl + dzl, nzl) * nx + lax.rem(x + dx, nx)) * nc + lax.rem(c + dc, nc)
        o = lax.rem(zh + dzh, nzh) * ny + lax.rem(y + dy, ny)
        return (f, o)

    def along_z(d):
        z = lax.rem(zh * nzl + zl + d, nzh * nzl)
        f = (lax.rem(z, nzl) * nx + x) * nc + c
        return (f, lax.div(z, nzl) * ny + y)

    started = []

    def copy(src, dst, rsem, to):
        cp = pltpu.make_async_remote_copy(
            src_ref=src, dst_ref=dst, send_sem=sent, recv_sem=rsem,
            device_id=to, device_id_type=MESH,
        )
        cp.start()
        started.append(cp)
        return cp

    def landed(like, sem):
        pltpu.make_async_copy(like, like, sem).wait()

    run = [(dz, dc) for dz in range(nzl) for dc in range(nc)]
    plane = [(dx, dy) for dx in range(nx) for dy in range(ny) if dx or dy]

    loads = []
    for dz in range(nzl):
        to_zl = lax.rem(zl + dz, nzl)
        load = pltpu.make_async_copy(slab.at[:, to_zl], stage.at[dz], load_sem.at[dz])
        load.start()
        loads.append(load)
    barrier = pltpu.get_barrier_semaphore()
    block_peers = [
        (dy, dz, dc) for dy in range(ny) for dz in range(nzl) for dc in range(nc) if dy or dz or dc
    ]
    line_of = range(1, nzl * nzh)
    chained = nzl == 4 and nzh == 4
    peers = [device(dzl=dz, dc=dc, dy=dy) for dy, dz, dc in block_peers if dy == 0 or not chained]
    peers += [device(dx=dx) for dx in range(1, nx)]
    if chained:
        step_one = [along_z(2), along_z(14), device(dy=1), device(dy=ny - 1)]
        step_two = [along_z(4), along_z(12), device(dy=1), device(dy=ny - 1)]
        peers += step_one
    else:
        peers += [along_z(d) for d in line_of]
    for peer in peers:
        pl.semaphore_signal(barrier, inc=1, device_id=peer, device_id_type=MESH)

    for k in range(nx):
        load = pltpu.make_async_copy(start.at[:, k], basis.at[k], load_sem.at[nzl + k])
        load.start()
        loads.append(load)

    def block(dx, dz, dc):
        b = (lax.rem(x + dx, nx) * nzl + lax.rem(zl + nzl - dz, nzl)) * nc + lax.rem(c + nc - dc, nc)
        return flat.at[pl.ds(pl.multiple_of(b * rows, rows), rows), :]

    def quarter(dx):
        return pl.ds(pl.multiple_of(lax.rem(x + dx, nx) * wide, wide), wide)

    here = block(0, 0, 0)
    keep = pltpu.make_async_copy(send.at[0, 0], here, load_sem.at[nzl + nx])
    for dz in range(nzl):
        loads[dz].wait()
        for px in range(nx):
            v0 = stage[dz, :, px * nc, :]
            v1 = stage[dz, :, px * nc + 1, :]
            send[dz, 0, :, px * CELLS : (px + 1) * CELLS] = jnp.where(c == 0, v0, v1).astype(BF16)
            send[dz, 1, :, px * CELLS : (px + 1) * CELLS] = jnp.where(c == 0, v1, v0).astype(BF16)
        if dz == 0:
            keep.start()
            pl.semaphore_wait(barrier, len(peers))
            if chained:
                for peer in step_one:
                    pl.semaphore_signal(near_sem, inc=1, device_id=peer, device_id_type=MESH)
        for dc in range(nc):
            if dz or dc:
                copy(send.at[dz, dc], here, a_in.at[dz, dc], device(dzl=dz, dc=dc))
        if dz == 0:
            copy(send.at[0, 0], here, x_in.at[0], device(dx=1))
            copy(send.at[0, 0], here, x_in.at[1], device(dx=nx - 1))
    for p in run[1:]:
        piece = block(0, *p)
        landed(piece, a_in.at[p])
        copy(piece, piece, x_in.at[0], device(dx=1))
        copy(piece, piece, x_in.at[1], device(dx=nx - 1))
    if chained:
        pl.semaphore_wait(near_sem, len(step_one))
        for peer in step_two:
            pl.semaphore_signal(far_sem, inc=1, device_id=peer, device_id_type=MESH)
    keep.wait()
    for load in loads[nzl:]:
        load.wait()

    def against(a, b):
        return lax.dot_general(a, b, (((1,), (1,)), ((), ())), preferred_element_type=F32)

    tops = jnp.concatenate([
        flat[pl.ds(pl.multiple_of(((x * nzl + q) * nc + k) * rows, rows), rows), :]
        for k in range(nc) for q in range(nzl)
    ], axis=0)

    def gram(d):
        part[d] = against(tops, flat[quarter(d), :]).reshape(part.shape[1:])
        copy(part.at[d, 1 - c], from_core.at[d], c_in.at[d], device(dc=1))

    def after_core(d):
        landed(from_core.at[d], c_in.at[d])
        for dy in (2, 1, 3, 0):
            q = lax.rem(y + dy, ny)
            if dy == 0:
                from_y[d, y] = part[d, c, q] + from_core[d, q]
            else:
                summed[d, q] = part[d, c, q] + from_core[d, q]
                copy(summed.at[d, q], from_y.at[d, y], y_in.at[d], device(dy=dy))

    def after_y(d):
        landed(from_y.at[d, 1:], y_in.at[d])
        chunks[d] = sum(from_y[d, q] for q in range(ny)).reshape(chunks.shape[1:])
        from_zl[d, zl] = chunks[d, zl]
        for dz in range(1, nzl):
            copy(chunks.at[d, lax.rem(zl + dz, nzl)], from_zl.at[d, zl], zl_in.at[d], device(dzl=dz))

    def after_zl(d):
        landed(from_zl.at[d, 1:], zl_in.at[d])
        from_zh[d, zh] = sum(from_zl[d, q] for q in range(nzl))
        for dz in range(1, nzh):
            copy(from_zh.at[d, zh], from_zh.at[d, zh], zh_in.at[d], device(dzh=dz))

    def after_zh(d):
        landed(from_zh.at[d, 1:], zh_in.at[d])
        own[d, zl] = sum(from_zh[d, q] for q in range(nzh))
        for dz in range(1, nzl):
            copy(own.at[d, zl], own.at[d, zl], o_in, device(dzl=dz))

    def weigh(d):
        return lax.dot_general(
            basis[lax.rem(x + d, nx)].reshape(wide, RANK), flat[quarter(d), :],
            (((0,), (0,)), ((), ())), preferred_element_type=F32,
        )

    def relay(d, core, dx):
        for q in range(nzl):
            b = (lax.rem(x + d, nx) * nzl + q) * nc + core
            piece = flat.at[pl.ds(pl.multiple_of(b * rows, rows), rows), :]
            copy(piece, piece, x_in.at[2], device(dx=dx))

    gram(0)
    landed(flat.at[quarter(nx - 1), :], x_in.at[0])
    relay(nx - 1, 0, 1)
    landed(flat.at[quarter(1), :], x_in.at[1])
    relay(1, 1, nx - 1)
    gram(3)
    gram(1)
    inner = weigh(0) + weigh(3) + weigh(1)
    after_core(0)
    after_core(3)
    after_core(1)
    after_y(0)
    if chained:
        pl.semaphore_wait(far_sem, len(step_two))
    landed(flat.at[quarter(2), :], x_in.at[2])

    gram(2)
    inner = inner + weigh(2)
    first_image = sum(against(tops, t) for t in thirds(inner)[::-1])
    small[...] = first_image.reshape(small.shape)
    s_in[0] = small[c, y, zl]
    reach = lambda p: min(p[0], ny - p[0]) + min(p[1], nzl - p[1])
    for n, (dy, dz, dc) in sorted(enumerate(block_peers), key=lambda p: -reach(p[1])):
        src = small.at[lax.rem(c + dc, nc), lax.rem(y + dy, ny), lax.rem(zl + dz, nzl)]
        copy(src, s_in.at[n + 1], si_in, device(dzl=dz, dc=dc, dy=dy))
    after_core(2)
    after_y(3)
    after_y(1)
    after_zl(0)
    after_y(2)

    landed(s_in.at[1:], si_in)
    place_z = zh * nzl + zl
    s_line[place_z] = jnp.sum(s_in[...], axis=0)
    for d in sorted(line_of, key=lambda d: -min(d, nzl * nzh - d)):
        copy(s_line.at[place_z], s_line.at[place_z], sl_in, along_z(d))
    after_zl(2)
    after_zl(3)
    after_zl(1)

    line = nzl * CHUNK

    def hops(p):
        return min(p[0], nx - p[0]) + min(p[1], ny - p[1])

    def group_of(p):
        return min(p[0], nx - p[0])

    def gather_spread(k):
        src = images.at[k, x, y, c]
        for p in sorted(plane, key=lambda p: (-group_of(p), -hops(p))):
            copy(src, src, p_in.at[k, group_of(p)], device(dx=p[0], dy=p[1]))

    def gather_pass(k, group):
        like = (images.at[k, 0, 1:, 0], images.at[k, 0:2, :, 0], images.at[k, 0, :, 0])[group]
        landed(like, p_in.at[k, group])
        for dx in range(nx):
            if group_of((dx, 0)) == group:
                src = images.at[k, lax.rem(x + dx, nx), :, c]
                copy(src, src, q_in.at[k], device(dc=1))

    def gather_end(k):
        landed(images.at[k, :, :, 0], q_in.at[k])

    def factor(k0, k1):
        lax.fori_loop(k0, k1, lambda b, _: (panel_step(b, work, inverse), 0)[1], 0)

    landed(s_line.at[1:], sl_in)
    images[0, x, y, c] = sum(
        s_line[q * nzl : (q + 1) * nzl] for q in range(nzh)
    ).reshape(line, RANK)
    gather_spread(0)
    after_zh(0)
    after_zh(3)
    after_zh(1)
    gather_pass(0, 0)
    gather_pass(0, 1)
    after_zh(2)
    gather_pass(0, 2)
    gather_end(0)
    image[...] = to_unit(images[0].reshape(image.shape))

    def times(strip, d):
        return jnp.dot(strip, image[quarter(d), :], preferred_element_type=F32, precision=lax.Precision.HIGHEST)

    landed(own.at[:, 1:], o_in)
    for k in range(1, ITERS):
        images[k, x, y, c] = sum(times(own[d].reshape(line, wide), d) for d in range(nx))
        gather_spread(k)
        start_factor(image[...], work)
        factor(0, 5)
        gather_pass(k, 0)
        gather_pass(k, 1)
        factor(5, RANK // PANEL)
        gather_pass(k, 2)
        gather_end(k)
        image[...] = to_unit(lax.dot_general(
            images[k].reshape(image.shape), inverse[...], (((1,), (1,)), ((), ())),
            preferred_element_type=F32, precision=lax.Precision.HIGHEST,
        ))
    start_factor(image[...], work)
    for b in range(RANK // PANEL):
        panel_step(b, work, inverse)
    for cp in started:
        cp.wait_send()
    narrow = lax.dot_general(
        image[...], inverse[...], (((1,), (1,)), ((), ())),
        preferred_element_type=F32, precision=lax.Precision.HIGHEST,
    ).astype(BF16)
    out[...] = lax.dot_general(
        narrow, flat[:, pl.ds(pl.multiple_of(x * CELLS, CELLS), CELLS)],
        (((0,), (0,)), ((), ())), preferred_element_type=F32,
    )


def local(grid, slab, start):
    nzl, nx, nc, nzh, ny = (grid[k] for k in ("zl", "x", "c", "zh", "y"))
    rows = slab.shape[0]
    order = start.shape[0]
    wide = order // nx
    deep = nzl * rows // ny
    dma = pltpu.SemaphoreType.DMA
    vmem = pltpu.VMEM
    core = pl.pallas_call(
        functools.partial(kernel, grid),
        out_shape=jax.ShapeDtypeStruct((RANK, CELLS), F32),
        in_specs=[pl.BlockSpec(memory_space=pltpu.HBM)] * 2,
        out_specs=pl.BlockSpec(memory_space=pltpu.VMEM),
        scratch_shapes=[
            vmem((nzl, rows, nx * nc, CELLS), F32),
            vmem((nx, nzl, nc * rows, RANK), BF16),
            vmem((nzl, nc, rows, nx * CELLS), BF16),
            vmem((order, nx * CELLS), BF16),
            vmem((nx, nc, ny, deep, wide), F32),
            vmem((nx, ny, deep, wide), F32),
            vmem((nx, ny, deep, wide), F32),
            vmem((nx, ny, deep, wide), F32),
            vmem((nx, nzl, CHUNK, wide), F32),
            vmem((nx, nzl, CHUNK, wide), F32),
            vmem((nx, nzh, CHUNK, wide), F32),
            vmem((nx, nzl, CHUNK, wide), F32),
            vmem((nc, ny, nzl, CHUNK, RANK), F32),
            vmem((nc * ny * nzl, CHUNK, RANK), F32),
            vmem((nzh * nzl, CHUNK, RANK), F32),
            vmem((order, RANK), F32),
            vmem((ITERS, nx, ny, nc, nzl * CHUNK, RANK), F32),
            vmem((RANK, 2 * RANK), F32),
            vmem((RANK, RANK), F32),
            dma((nzl + nx + 1,)), dma(()),
            dma((nzl, nc)), dma((3,)), dma((nx,)), dma((nx,)), dma((nx,)), dma((nx,)),
            dma(()), dma(()), dma(()), dma((ITERS, 3)), dma((ITERS,)),
            pltpu.SemaphoreType.REGULAR, pltpu.SemaphoreType.REGULAR,
        ],
        compiler_params=pltpu.CompilerParams(
            collective_id=0, has_side_effects=True, vmem_limit_bytes=55104 * 2**10
        ),
        name="truncate",
    )(slab.reshape(rows, nzl, nx * nc, CELLS), start.reshape(nzl, nx, nc * rows, RANK))
    return core.reshape(RANK, 1, 1, CELLS)


def solution(mesh, grid=GRID):
    placed = (P("fib", "oth", None, None), P())
    return jax.shard_map(
        functools.partial(local, grid), mesh=mesh, in_specs=placed,
        out_specs=P(None, "oth", "fib", None), check_vma=False,
    )
```

```python
import functools

import jax
import jax.numpy as jnp
from jax import lax
from jax.experimental import pallas as pl
from jax.experimental.pallas import tpu as pltpu
from jax.sharding import PartitionSpec as P

ITERS = 3
RANK = 128
CELLS = 128
CHUNK = 8
GRID = dict(zl=4, x=4, c=2, zh=4, y=4)
MESH = pl.DeviceIdType.MESH
F32 = jnp.float32
BF16 = jnp.bfloat16


def thirds(a):
    high = a.astype(BF16)
    rest = a - high.astype(F32)
    mid = rest.astype(BF16)
    return high, mid, (rest - mid.astype(F32)).astype(BF16)


PANEL = 16
TILES = PANEL // 8


def panel_step(b, work, inverse):
    fixed = isinstance(b, int)
    base = b * PANEL if fixed else pl.multiple_of(b * PANEL, PANEL)
    left = work[pl.ds(base, PANEL), 0:RANK]
    right = work[pl.ds(base, PANEL), RANK : 2 * RANK]
    turned, at = (left, base) if fixed else (pltpu.roll(left, RANK - base, 1), 0)
    row = lax.broadcasted_iota(jnp.int32, (8, RANK), 0)
    tiles = []
    for t in range(TILES):
        rows = slice(8 * t, 8 * t + 8)
        cols = [jnp.broadcast_to(turned[rows, at + s : at + s + 1], (8, RANK)) for s in range(PANEL)]
        tiles.append(jnp.stack(cols + [left[rows], right[rows]]))
    pivots = [jnp.ones((8, RANK), F32) for _ in range(TILES)]
    for s in range(PANEL):
        ts, ss = divmod(s, 8)
        pivot = jnp.broadcast_to(tiles[ts][0, ss : ss + 1, :], (8, RANK))
        pivots[ts] = jnp.where(row == ss, pivot, pivots[ts])
        over = 1.0 / pivot
        lead = jnp.broadcast_to(tiles[ts][1:, ss : ss + 1, :], (PANEL + 1 - s, 8, RANK))
        for t in range(TILES):
            rest = tiles[t][1:]
            if t >= ts:
                factor = tiles[t][0] * over
                if t == ts:
                    factor = jnp.where(row > ss, factor, 0.0)
                rest = rest - factor[None] * lead
            tiles[t] = rest
    left = jnp.concatenate([tile[0] for tile in tiles], axis=0)
    right = jnp.concatenate([tile[1] for tile in tiles], axis=0)
    pivots = jnp.concatenate(pivots, axis=0)
    inverse[pl.ds(base, PANEL), :] = right * lax.rsqrt(pivots)
    if fixed and base + PANEL == RANK:
        return
    lane = lax.broadcasted_iota(jnp.int32, (PANEL, RANK), 1)
    factors = jnp.where(lane >= base + PANEL, left * (1.0 / pivots), 0.0)
    fh, fm, fl = thirds(factors)
    rh, rm, rl = thirds(jnp.concatenate([left, right], axis=1))
    tall = jnp.concatenate([fh, fh, fm, fh, fl, fm], axis=0)
    wide = jnp.concatenate([rh, rm, rh, rl, rh, rm], axis=0)
    change = lax.dot_general(tall, wide, (((0,), (0,)), ((), ())), preferred_element_type=F32)
    if fixed:
        work[base + PANEL :, :] = work[base + PANEL :, :] - change[base + PANEL :]
    else:
        work[...] = work[...] - change


def start_factor(image, work):
    work[:, 0:RANK] = lax.dot_general(
        image, image, (((0,), (0,)), ((), ())),
        preferred_element_type=F32, precision=lax.Precision.HIGHEST,
    )
    i0 = lax.broadcasted_iota(jnp.int32, (RANK, RANK), 0)
    i1 = lax.broadcasted_iota(jnp.int32, (RANK, RANK), 1)
    work[:, RANK : 2 * RANK] = (i0 == i1).astype(F32)


def to_unit(image):
    return image * (1.0 / jnp.max(jnp.abs(image)))


def kernel(
    grid, slab, start, out,
    stage, basis, send, flat, part, from_core, summed, from_y, chunks, from_zl, from_zh, own,
    small, s_in, s_line, image, images, work, inverse,
    load_sem, sent, a_in, x_in, c_in, y_in, zl_in, zh_in, o_in, si_in, sl_in, p_in, q_in, near_sem, far_sem,
):
    nzl, nx, nc, nzh, ny = (grid[k] for k in ("zl", "x", "c", "zh", "y"))
    rows = stage.shape[1]
    wide = part.shape[4]
    fib, oth = lax.axis_index("fib"), lax.axis_index("oth")
    c = lax.rem(fib, nc)
    x = lax.rem(lax.div(fib, nc), nx)
    zl = lax.div(fib, nc * nx)
    y = lax.rem(oth, ny)
    zh = lax.div(oth, ny)

    def device(dzl=0, dx=0, dc=0, dzh=0, dy=0):
        f = (lax.rem(zl + dzl, nzl) * nx + lax.rem(x + dx, nx)) * nc + lax.rem(c + dc, nc)
        o = lax.rem(zh + dzh, nzh) * ny + lax.rem(y + dy, ny)
        return (f, o)

    def along_z(d):
        z = lax.rem(zh * nzl + zl + d, nzh * nzl)
        f = (lax.rem(z, nzl) * nx + x) * nc + c
        return (f, lax.div(z, nzl) * ny + y)

    started = []

    def copy(src, dst, rsem, to):
        cp = pltpu.make_async_remote_copy(
            src_ref=src, dst_ref=dst, send_sem=sent, recv_sem=rsem,
            device_id=to, device_id_type=MESH,
        )
        cp.start()
        started.append(cp)
        return cp

    def landed(like, sem):
        pltpu.make_async_copy(like, like, sem).wait()

    run = [(dz, dc) for dz in range(nzl) for dc in range(nc)]
    plane = [(dx, dy) for dx in range(nx) for dy in range(ny) if dx or dy]

    loads = []
    for dz in range(nzl):
        to_zl = lax.rem(zl + dz, nzl)
        load = pltpu.make_async_copy(slab.at[:, to_zl], stage.at[dz], load_sem.at[dz])
        load.start()
        loads.append(load)
    barrier = pltpu.get_barrier_semaphore()
    block_peers = [
        (dy, dz, dc) for dy in range(ny) for dz in range(nzl) for dc in range(nc) if dy or dz or dc
    ]
    line_of = range(1, nzl * nzh)
    chained = nzl == 4 and nzh == 4
    peers = [device(dzl=dz, dc=dc, dy=dy) for dy, dz, dc in block_peers if dy == 0 or not chained]
    peers += [device(dx=dx) for dx in range(1, nx)]
    if chained:
        step_one = [along_z(2), along_z(14), device(dy=1), device(dy=ny - 1)]
        step_two = [along_z(4), along_z(12), device(dy=1), device(dy=ny - 1)]
        peers += step_one
    else:
        peers += [along_z(d) for d in line_of]
    for peer in peers:
        pl.semaphore_signal(barrier, inc=1, device_id=peer, device_id_type=MESH)

    for k in range(nx):
        load = pltpu.make_async_copy(start.at[:, k], basis.at[k], load_sem.at[nzl + k])
        load.start()
        loads.append(load)

    def block(dx, dz, dc):
        b = (lax.rem(x + dx, nx) * nzl + lax.rem(zl + nzl - dz, nzl)) * nc + lax.rem(c + nc - dc, nc)
        return flat.at[pl.ds(pl.multiple_of(b * rows, rows), rows), :]

    def quarter(dx):
        return pl.ds(pl.multiple_of(lax.rem(x + dx, nx) * wide, wide), wide)

    here = block(0, 0, 0)
    keep = pltpu.make_async_copy(send.at[0, 0], here, load_sem.at[nzl + nx])
    for dz in range(nzl):
        loads[dz].wait()
        for px in range(nx):
            v0 = stage[dz, :, px * nc, :]
            v1 = stage[dz, :, px * nc + 1, :]
            send[dz, 0, :, px * CELLS : (px + 1) * CELLS] = jnp.where(c == 0, v0, v1).astype(BF16)
            send[dz, 1, :, px * CELLS : (px + 1) * CELLS] = jnp.where(c == 0, v1, v0).astype(BF16)
        if dz == 0:
            keep.start()
            pl.semaphore_wait(barrier, len(peers))
            if chained:
                for peer in step_one:
                    pl.semaphore_signal(near_sem, inc=1, device_id=peer, device_id_type=MESH)
        for dc in range(nc):
            if dz or dc:
                copy(send.at[dz, dc], here, a_in.at[dz, dc], device(dzl=dz, dc=dc))
        if dz == 0:
            copy(send.at[0, 0], here, x_in.at[0], device(dx=1))
            copy(send.at[0, 0], here, x_in.at[1], device(dx=nx - 1))
    for p in run[1:]:
        piece = block(0, *p)
        landed(piece, a_in.at[p])
        copy(piece, piece, x_in.at[0], device(dx=1))
        copy(piece, piece, x_in.at[1], device(dx=nx - 1))
    if chained:
        pl.semaphore_wait(near_sem, len(step_one))
        for peer in step_two:
            pl.semaphore_signal(far_sem, inc=1, device_id=peer, device_id_type=MESH)
    keep.wait()
    for load in loads[nzl:]:
        load.wait()

    def against(a, b):
        return lax.dot_general(a, b, (((1,), (1,)), ((), ())), preferred_element_type=F32)

    tops = jnp.concatenate([
        flat[pl.ds(pl.multiple_of(((x * nzl + q) * nc + k) * rows, rows), rows), :]
        for k in range(nc) for q in range(nzl)
    ], axis=0)

    def gram(d):
        part[d] = against(tops, flat[quarter(d), :]).reshape(part.shape[1:])
        copy(part.at[d, 1 - c], from_core.at[d], c_in.at[d], device(dc=1))

    def after_core(d):
        landed(from_core.at[d], c_in.at[d])
        for dy in (2, 1, 3, 0):
            q = lax.rem(y + dy, ny)
            if dy == 0:
                from_y[d, y] = part[d, c, q] + from_core[d, q]
            else:
                summed[d, q] = part[d, c, q] + from_core[d, q]
                copy(summed.at[d, q], from_y.at[d, y], y_in.at[d], device(dy=dy))

    def after_y(d):
        landed(from_y.at[d, 1:], y_in.at[d])
        chunks[d] = sum(from_y[d, q] for q in range(ny)).reshape(chunks.shape[1:])
        from_zl[d, zl] = chunks[d, zl]
        for dz in range(1, nzl):
            copy(chunks.at[d, lax.rem(zl + dz, nzl)], from_zl.at[d, zl], zl_in.at[d], device(dzl=dz))

    def after_zl(d):
        landed(from_zl.at[d, 1:], zl_in.at[d])
        from_zh[d, zh] = sum(from_zl[d, q] for q in range(nzl))
        for dz in range(1, nzh):
            copy(from_zh.at[d, zh], from_zh.at[d, zh], zh_in.at[d], device(dzh=dz))

    def after_zh(d):
        landed(from_zh.at[d, 1:], zh_in.at[d])
        own[d, zl] = sum(from_zh[d, q] for q in range(nzh))
        for dz in range(1, nzl):
            copy(own.at[d, zl], own.at[d, zl], o_in, device(dzl=dz))

    def weigh(d):
        return lax.dot_general(
            basis[lax.rem(x + d, nx)].reshape(wide, RANK), flat[quarter(d), :],
            (((0,), (0,)), ((), ())), preferred_element_type=F32,
        )

    def relay(d, core, dx):
        for q in range(nzl):
            b = (lax.rem(x + d, nx) * nzl + q) * nc + core
            piece = flat.at[pl.ds(pl.multiple_of(b * rows, rows), rows), :]
            copy(piece, piece, x_in.at[2], device(dx=dx))

    gram(0)
    landed(flat.at[quarter(nx - 1), :], x_in.at[0])
    relay(nx - 1, 0, 1)
    landed(flat.at[quarter(1), :], x_in.at[1])
    relay(1, 1, nx - 1)
    gram(3)
    gram(1)
    inner = weigh(0) + weigh(3) + weigh(1)
    after_core(0)
    after_core(3)
    after_core(1)
    after_y(0)
    if chained:
        pl.semaphore_wait(far_sem, len(step_two))
    landed(flat.at[quarter(2), :], x_in.at[2])

    gram(2)
    inner = inner + weigh(2)
    first_image = sum(against(tops, t) for t in thirds(inner)[::-1])
    small[...] = first_image.reshape(small.shape)
    s_in[0] = small[c, y, zl]
    reach = lambda p: min(p[0], ny - p[0]) + min(p[1], nzl - p[1])
    for n, (dy, dz, dc) in sorted(enumerate(block_peers), key=lambda p: -reach(p[1])):
        src = small.at[lax.rem(c + dc, nc), lax.rem(y + dy, ny), lax.rem(zl + dz, nzl)]
        copy(src, s_in.at[n + 1], si_in, device(dzl=dz, dc=dc, dy=dy))
    after_core(2)
    after_y(3)
    after_y(1)
    after_zl(0)
    after_y(2)

    landed(s_in.at[1:], si_in)
    place_z = zh * nzl + zl
    s_line[place_z] = jnp.sum(s_in[...], axis=0)
    for d in sorted(line_of, key=lambda d: -min(d, nzl * nzh - d)):
        copy(s_line.at[place_z], s_line.at[place_z], sl_in, along_z(d))
    after_zl(2)
    after_zl(3)
    after_zl(1)

    line = nzl * CHUNK

    def hops(p):
        return min(p[0], nx - p[0]) + min(p[1], ny - p[1])

    def group_of(p):
        return min(p[0], nx - p[0])

    def gather_spread(k):
        src = images.at[k, x, y, c]
        for p in sorted(plane, key=lambda p: (-group_of(p), -hops(p))):
            copy(src, src, p_in.at[k, group_of(p)], device(dx=p[0], dy=p[1]))

    def gather_pass(k, group):
        like = (images.at[k, 0, 1:, 0], images.at[k, 0:2, :, 0], images.at[k, 0, :, 0])[group]
        landed(like, p_in.at[k, group])
        for dx in range(nx):
            if group_of((dx, 0)) == group:
                src = images.at[k, lax.rem(x + dx, nx), :, c]
                copy(src, src, q_in.at[k], device(dc=1))

    def gather_end(k):
        landed(images.at[k, :, :, 0], q_in.at[k])

    def factor(k0, k1):
        for b in range(k0, k1):
            panel_step(b, work, inverse)

    landed(s_line.at[1:], sl_in)
    images[0, x, y, c] = sum(
        s_line[q * nzl : (q + 1) * nzl] for q in range(nzh)
    ).reshape(line, RANK)
    gather_spread(0)
    after_zh(0)
    after_zh(3)
    after_zh(1)
    gather_pass(0, 0)
    gather_pass(0, 1)
    after_zh(2)
    gather_pass(0, 2)
    gather_end(0)
    image[...] = to_unit(images[0].reshape(image.shape))

    def times(strip, d):
        return jnp.dot(strip, image[quarter(d), :], preferred_element_type=F32, precision=lax.Precision.HIGHEST)

    landed(own.at[:, 1:], o_in)
    for k in range(1, ITERS):
        images[k, x, y, c] = sum(times(own[d].reshape(line, wide), d) for d in range(nx))
        gather_spread(k)
        start_factor(image[...], work)
        factor(0, 5)
        gather_pass(k, 0)
        gather_pass(k, 1)
        factor(5, RANK // PANEL)
        gather_pass(k, 2)
        gather_end(k)
        image[...] = to_unit(lax.dot_general(
            images[k].reshape(image.shape), inverse[...], (((1,), (1,)), ((), ())),
            preferred_element_type=F32, precision=lax.Precision.HIGHEST,
        ))
    start_factor(image[...], work)
    for b in range(RANK // PANEL):
        panel_step(b, work, inverse)
    for cp in started:
        cp.wait_send()
    narrow = lax.dot_general(
        image[...], inverse[...], (((1,), (1,)), ((), ())),
        preferred_element_type=F32, precision=lax.Precision.HIGHEST,
    ).astype(BF16)
    out[...] = lax.dot_general(
        narrow, flat[:, pl.ds(pl.multiple_of(x * CELLS, CELLS), CELLS)],
        (((0,), (0,)), ((), ())), preferred_element_type=F32,
    )


def local(grid, slab, start):
    nzl, nx, nc, nzh, ny = (grid[k] for k in ("zl", "x", "c", "zh", "y"))
    rows = slab.shape[0]
    order = start.shape[0]
    wide = order // nx
    deep = nzl * rows // ny
    dma = pltpu.SemaphoreType.DMA
    vmem = pltpu.VMEM
    core = pl.pallas_call(
        functools.partial(kernel, grid),
        out_shape=jax.ShapeDtypeStruct((RANK, CELLS), F32),
        in_specs=[pl.BlockSpec(memory_space=pltpu.HBM)] * 2,
        out_specs=pl.BlockSpec(memory_space=pltpu.VMEM),
        scratch_shapes=[
            vmem((nzl, rows, nx * nc, CELLS), F32),
            vmem((nx, nzl, nc * rows, RANK), BF16),
            vmem((nzl, nc, rows, nx * CELLS), BF16),
            vmem((order, nx * CELLS), BF16),
            vmem((nx, nc, ny, deep, wide), F32),
            vmem((nx, ny, deep, wide), F32),
            vmem((nx, ny, deep, wide), F32),
            vmem((nx, ny, deep, wide), F32),
            vmem((nx, nzl, CHUNK, wide), F32),
            vmem((nx, nzl, CHUNK, wide), F32),
            vmem((nx, nzh, CHUNK, wide), F32),
            vmem((nx, nzl, CHUNK, wide), F32),
            vmem((nc, ny, nzl, CHUNK, RANK), F32),
            vmem((nc * ny * nzl, CHUNK, RANK), F32),
            vmem((nzh * nzl, CHUNK, RANK), F32),
            vmem((order, RANK), F32),
            vmem((ITERS, nx, ny, nc, nzl * CHUNK, RANK), F32),
            vmem((RANK, 2 * RANK), F32),
            vmem((RANK, RANK), F32),
            dma((nzl + nx + 1,)), dma(()),
            dma((nzl, nc)), dma((3,)), dma((nx,)), dma((nx,)), dma((nx,)), dma((nx,)),
            dma(()), dma(()), dma(()), dma((ITERS, 3)), dma((ITERS,)),
            pltpu.SemaphoreType.REGULAR, pltpu.SemaphoreType.REGULAR,
        ],
        compiler_params=pltpu.CompilerParams(
            collective_id=0, has_side_effects=True, vmem_limit_bytes=55104 * 2**10
        ),
        name="truncate",
    )(slab.reshape(rows, nzl, nx * nc, CELLS), start.reshape(nzl, nx, nc * rows, RANK))
    return core.reshape(RANK, 1, 1, CELLS)


def solution(mesh, grid=GRID):
    placed = (P("fib", "oth", None, None), P())
    return jax.shard_map(
        functools.partial(local, grid), mesh=mesh, in_specs=placed,
        out_specs=P(None, "oth", "fib", None), check_vma=False,
    )
```
